128 devices in a mesh: seq: 8 (over x, z_lo), dp: 16 (over z_hi, y, core).
Axes of the slice: x: 4, y: 4, z: 4 (z_hi: 2, z_lo: 2; z = z_hi * 2 + z_lo), core: 2. Of those that a mesh axis runs over, the one named last changes fastest.
Arguments:
- query_in: bfloat16 [16, 32, 64, 1536], P('dp', 'seq'), may hold values from -8 to 8
- key_in: bfloat16 [16, 32, 64, 1536], P('dp', 'seq'), may hold values from -8 to 8
- value_in: bfloat16 [16, 32, 64, 1536], P('dp', 'seq'), may hold values from -5 to 5
- cotangent: bfloat16 [16, 32, 64, 3072], P('dp', 'seq'), may hold values from -5 to 5
- out_weight: bfloat16 [1536, 3072], P(('seq', 'dp')), may hold values from -0.15625 to 0.15625
Outputs:
- grad_query: bfloat16 [16, 32, 64, 1536], P('dp', 'seq')
- grad_key: bfloat16 [16, 32, 64, 1536], P('dp', 'seq')
- grad_value: bfloat16 [16, 32, 64, 1536], P('dp', 'seq')
- grad_weight: float32 [1536, 3072], P(('seq', 'dp'))
The draws below stay inside these ranges and needn't reach their ends.
All inputs are finite; a program needn't handle non-finite values.
Results may differ from the reference program's by a relative error of at most 0.0073.
Values may be sent and summed in bfloat16 or wider, within the bound.
A program may use at most 128 MiB of HBM per device.

```python
import math
import jax
import jax.numpy as jnp
from jax import lax

D = 3072
HEADS = 12
HDIM = 128
FRAMES = 32
SPACE = 64
CLIPS = 16
HD = 1536
TOKENS_ALL = 32768


def draw_query_in(key, part):
    key = jax.random.fold_in(key, 3)
    full_shape = (CLIPS, FRAMES, SPACE, HEADS, HDIM)
    draw_base = jnp.clip(jax.random.normal(key, full_shape, jnp.float32), -4.0, 4.0)
    return draw_base.reshape(CLIPS, FRAMES, SPACE, HEADS * HDIM).astype(jnp.bfloat16)


def draw_key_in(key, part):
    key = jax.random.fold_in(key, 7)
    full_shape = (CLIPS, FRAMES, SPACE, HEADS, HDIM)
    draw_base = jnp.clip(jax.random.normal(key, full_shape, jnp.float32), -4.0, 4.0)
    return draw_base.reshape(CLIPS, FRAMES, SPACE, HEADS * HDIM).astype(jnp.bfloat16)


def block_levels(stream_key, dims, cuts, least, largest):
    factor_of, own = 1.0, jax.random.fold_in(stream_key, 6)
    for axis_at, shards_of in cuts:
        steps = jnp.exp(jax.random.uniform(jax.random.fold_in(own, axis_at), (shards_of,), jnp.float32, least / len(cuts), largest / len(cuts)))
        factor_of = factor_of * jnp.repeat(steps, dims[axis_at] // shards_of).reshape([-1 if axis == axis_at else 1 for axis in range(len(dims))])
    return factor_of


def scatter_about(own_key, dims, deviation, most, cuts=(), held_as=jnp.bfloat16):
    drawn = jax.random.normal(own_key, dims, jnp.float32) * deviation
    if len(cuts) > 0:
        drawn = block_levels(own_key, dims, cuts, -0.22, 0.18) * drawn
    return jnp.clip(drawn, min=-most, max=most).astype(held_as)


def setup_inputs(seed: int = 0) -> dict:
    seeds = jax.random.split(jax.random.key(seed), 6)
    query_in = draw_query_in(jax.random.fold_in(seeds[5], 71), 0)
    key_in = draw_key_in(jax.random.fold_in(seeds[5], 71), 0)
    value_in = scatter_about(seeds[2], (CLIPS, FRAMES, SPACE, HD), 1.0, 5.0, ((0, 16), (1, 8)))
    cotangent = scatter_about(seeds[3], (CLIPS, FRAMES, SPACE, D), 1.0, 5.0, ((0, 16), (1, 8)))
    out_weight = scatter_about(seeds[4], (HD, D), HD ** -0.5, 0.15625, ((0, 128),))
    return dict(query_in=query_in, key_in=key_in, value_in=value_in, cotangent=cotangent, out_weight=out_weight)


def clip_grads(query_in, key_in, value_in, cotangent, out_weight):
    score_scale = 1.0 / math.sqrt(HDIM)
    query_h = query_in.reshape(FRAMES, SPACE, HEADS, HDIM).astype(jnp.float32)
    key_h = key_in.reshape(FRAMES, SPACE, HEADS, HDIM).astype(jnp.float32)
    value_h = value_in.reshape(FRAMES, SPACE, HEADS, HDIM).astype(jnp.float32)
    score = jnp.einsum('fshe,gshe->shfg', query_h, key_h) * score_scale
    attn_prob = jax.nn.softmax(score, axis=-1)
    prob_low = lax.optimization_barrier(attn_prob.astype(jnp.bfloat16)).astype(jnp.float32)
    attn_out = jnp.einsum('shfg,gshe->fshe', prob_low, value_h).astype(jnp.bfloat16)
    out_flat = attn_out.reshape(FRAMES * SPACE, HEADS * HDIM)
    cot_flat = cotangent.reshape(FRAMES * SPACE, D)
    d_out = jnp.dot(cot_flat, out_weight.T, preferred_element_type=jnp.float32).astype(jnp.bfloat16)
    weight_term = jnp.dot(out_flat.T, cot_flat, preferred_element_type=jnp.float32)
    d_head = d_out.reshape(FRAMES, SPACE, HEADS, HDIM).astype(jnp.float32)
    grad_value = jnp.einsum('shfg,fshe->gshe', prob_low, d_head).astype(jnp.bfloat16)
    d_prob = jnp.einsum('fshe,gshe->shfg', d_head, value_h)
    d_score = attn_prob * (d_prob - lax.optimization_barrier(jnp.sum(attn_prob * d_prob, axis=-1, keepdims=True)))
    score_low = lax.optimization_barrier(d_score.astype(jnp.bfloat16)).astype(jnp.float32)
    grad_query = (jnp.einsum('shfg,gshe->fshe', score_low, key_h) * score_scale).astype(jnp.bfloat16)
    grad_key = (jnp.einsum('shfg,fshe->gshe', score_low, query_h) * score_scale).astype(jnp.bfloat16)
    flat_shape = (FRAMES, SPACE, HEADS * HDIM)
    return (grad_query.reshape(flat_shape), grad_key.reshape(flat_shape), grad_value.reshape(flat_shape), weight_term)

def reference(query_in, key_in, value_in, cotangent, out_weight):

    def one_clip(total, inputs):
        grad_query, grad_key, grad_value, weight_term = clip_grads(inputs[0], inputs[1], inputs[2], inputs[3], out_weight)
        return (total + weight_term, (grad_query, grad_key, grad_value))
    start_total = jnp.zeros((HEADS * HDIM, D), jnp.float32)
    weight_sum, grads = lax.scan(one_clip, start_total, (query_in, key_in, value_in, cotangent))
    grad_weight = weight_sum * (1.0 / math.sqrt(TOKENS_ALL))
    return (grads[0], grads[1], grads[2], grad_weight)
```

```python
import math

import jax
import jax.numpy as jnp
from jax import lax
from jax.experimental import pallas as pl
from jax.experimental.pallas import tpu as pltpu
from jax.sharding import PartitionSpec as P

MESH = pl.DeviceIdType.MESH
F32, BF16 = jnp.float32, jnp.bfloat16

FRAMES, POS, HD, D, HDIM = 32, 16, 1536, 3072, 128
HALF = HD // 2
TOK = FRAMES * POS
HEADS = HALF // HDIM
PK = 2304
COL = 768
ROWS = 512
NAT = 384
NT = (((1,), (1,)), ((), ()))
TN = (((0,), (0,)), ((), ()))


def dot(a, b, dims=(((1,), (0,)), ((), ()))):
    return lax.dot_general(a, b, dims, preferred_element_type=F32)


def kernel(
    q_in, k_in, v_in, c_in, w_in,
    gq_out, gk_out, gv_out, gw_out,
    qb, kb, vb, cb, wp, wn, prob, ao, aot, em, um, part, ry, s1, rz, s2, rf, dob, gqb, gkb, gvb,
    a_ss, a_rs, f_ss, f_rs, w1_ss, w1_rs, w2_ss, w2_rs, w3_ss, w3_rs,
    y_ss, y_rs, z_ss, z_rs, x_ss, x_rs, g_ss, g_rs,
):
    seq, dp = lax.axis_index("seq"), lax.axis_index("dp")
    x, zl = seq // 2, seq % 2
    zh, y, c = dp // 8, (dp // 2) % 4, dp % 2
    z = zh * 2 + zl

    def dev(x, y, z, c):
        return {"seq": x * 2 + z % 2, "dp": (z // 2) * 8 + y * 2 + c}

    def remote(src, dst, ss, rs, to):
        return pltpu.make_async_remote_copy(
            src_ref=src, dst_ref=dst, send_sem=ss, recv_sem=rs, device_id=to, device_id_type=MESH
        )

    def done(ref, sem):
        pltpu.make_async_copy(ref, ref, sem).wait()

    def post(src, dst, ss, rs, to, own=None):
        if own is None:
            remote(src, dst, ss, rs, to).start()
            return

        @pl.when(own)
        def _():
            pltpu.make_async_copy(src, dst, rs).start()

        @pl.when(jnp.logical_not(own))
        def _():
            remote(src, dst, ss, rs, to).start()

    def sent(src, ss, own=None):
        if own is None:
            done(src, ss)
        else:
            pl.when(jnp.logical_not(own))(lambda: done(src, ss))

    barrier = pltpu.get_barrier_semaphore()
    peers = [
        dev((x + dx) % 4, y, zh * 2 + (zl + kz) % 2, (c + kc) % 2)
        for dx in range(4) for kz in range(2) for kc in range(2) if dx or kz or kc
    ]
    peers += [dev(x, y, (z + 2) % 4, c), dev(x, y, ((z + 2) % 4) // 2 * 2 + (zl + 1) % 2, c)]
    peers += [dev(x, (y + dy) % 4, z, c) for dy in range(1, 4)]
    for to in peers:
        pl.semaphore_signal(barrier, inc=1, device_id=to, device_id_type=MESH)
    pl.semaphore_wait(barrier, len(peers))

    half = x // 2
    w_own = c == half
    w_slot = wp.at[x % 2, y, z, pl.ds(pl.multiple_of(c * 16, 16), 16), :]

    def w1_args(dx):
        return (w_in, w_slot, w1_ss.at[dx], w1_rs.at[(x % 2) * 2 + c], dev((x + dx) % 4, y, z, half))

    for dx in range(4):
        post(*w1_args(dx), own=w_own if dx == 0 else None)

    a_own = zl == c
    mine = pl.ds(pl.multiple_of(seq * 4, 4), 4)

    def a_args(arr, dx, kc):
        px, core = (x + dx) % 4, (c + kc) % 2
        to = dev(px, y, zh * 2 + c, core)
        pos = pl.ds(pl.multiple_of(px * 16, 16), 16)
        if arr < 3:
            col = pl.ds(pl.multiple_of(core * HALF, HALF), HALF)
            src = (q_in, k_in, v_in)[arr].at[:, pos, col]
            dst = (qb, kb, vb)[arr].at[mine]
        else:
            col = pl.ds(pl.multiple_of(core * HD, HD), HD)
            src = c_in.at[:, pos, col]
            dst = cb.at[mine, :, col]
        return src, dst, a_ss.at[arr, dx * 2 + kc], a_rs.at[arr, seq], to

    def a_each(fn):
        for arr in range(4):
            for dx in (2, 1, 3, 0):
                for kc in range(2):
                    fn(arr, dx, kc, a_own if dx == 0 and kc == 0 else None)

    a_each(lambda arr, dx, kc, own: post(*a_args(arr, dx, kc), own=own))

    def packed(shape, axis):
        m = lax.broadcasted_iota(jnp.int32, shape, axis)
        j, r = m >> 4, m & 15
        owner = ((j >> 1) & 1) * 16 + ((j >> 2) & 1) * 8 + (j >> 3) * 2 + (j & 1)
        return owner * 12, r

    base, r = packed((ROWS, NAT), 0)
    n = lax.broadcasted_iota(jnp.int32, (ROWS, NAT), 1)
    for p in range(3):
        hit = n == jnp.where(r < 12, base + r, base + (r - 12 + 4 * p))
        em[p] = jnp.where(hit, 1.0, 0.0).astype(BF16)
    base, r = packed((NAT, ROWS), 1)
    n = lax.broadcasted_iota(jnp.int32, (NAT, ROWS), 0)
    um[0] = jnp.where(n == jnp.where(r < 12, base + r, -1), 1.0, 0.0).astype(BF16)
    for p in range(3):
        hit = n == jnp.where(r < 12, -1, base + (r - 12 + 4 * p))
        um[p + 1] = jnp.where(hit, 1.0, 0.0).astype(BF16)

    for i in range(4):
        done(wp.at[i // 2, y, z, pl.ds((i % 2) * 16, 16), :], w1_rs.at[i])

    def w2_args(dz):
        blk = wp.at[:, y, z]
        return (blk, blk, w2_ss.at[dz - 1], w2_rs.at[z], dev(x, y, (z + dz) % 4, c))

    for dz in range(1, 4):
        post(*w2_args(dz))

    def w3_args(dz, dy):
        zz = (z + dz) % 4
        blk = wp.at[:, y, zz]
        return (blk, blk, w3_ss.at[dz * 3 + dy - 1], w3_rs.at[y * 4 + zz], dev(x, (y + dy) % 4, z, c))

    for dz in (0, 1, 3, 2):
        if dz:
            zz = (z + dz) % 4
            done(wp.at[:, y, zz], w2_rs.at[zz])
        for dy in (2, 1, 3):
            post(*w3_args(dz, dy))

    for s in range(8):
        for arr, buf in enumerate((qb, kb, vb)):
            done(buf.at[pl.ds(s * 4, 4)], a_rs.at[arr, s])

    scale = 1.0 / math.sqrt(HDIM)

    def head(buf, h):
        return buf[:, :, pl.ds(pl.multiple_of(h * HDIM, HDIM), HDIM)].reshape(TOK, HDIM)

    def forward(h, _):
        score = dot(head(qb, h), head(kb, h), NT) * scale
        row = lax.broadcasted_iota(jnp.int32, (TOK, TOK), 0)
        col = lax.broadcasted_iota(jnp.int32, (TOK, TOK), 1)
        score = jnp.where(((row ^ col) & 15) == 0, score, -1e30)
        e = jnp.exp(score - jnp.max(score, axis=-1, keepdims=True))
        pr = e / jnp.sum(e, axis=-1, keepdims=True)
        prob[h] = pr
        out = dot(pr.astype(BF16), head(vb, h))
        ao[:, pl.ds(pl.multiple_of(h * HDIM, HDIM), HDIM)] = out.astype(BF16)
        return 0

    lax.fori_loop(0, HEADS, forward, 0)
    for g in range(2):
        for p in range(3):
            aot[p, g] = dot(em[p], ao[:, g * NAT : (g + 1) * NAT], NT).astype(BF16)

    own_col = pl.ds(pl.multiple_of(c * HD, HD), HD)
    twin_col = pl.ds(pl.multiple_of((1 - c) * HD, HD), HD)
    twin = dev(x, y, z, (c + 1) % 2)
    for s in range(8):
        blk = cb.at[pl.ds(s * 4, 4), :, own_col]
        done(blk, a_rs.at[3, s])
        post(blk, blk, f_ss.at[s], f_rs.at[s], twin)
    for s in range(8):
        done(cb.at[pl.ds(s * 4, 4), :, twin_col], f_rs.at[s])

    def y_args(p, dy):
        to = (y + dy) % 4
        return (part.at[p, to], ry.at[p, y], y_ss.at[p, dy - 1], y_rs.at[p, y], dev(x, to, z, c))

    keep = (lax.broadcasted_iota(jnp.int32, (ROWS, 256), 0) & 15) < 12
    for p in range(3):
        def grad(i, _, p=p):
            g, t = i // 3, i % 3
            a = aot[p, g]
            lo = cb[:, :, pl.ds(pl.multiple_of(p * COL + t * 256, 256), 256)].reshape(TOK, 256)
            hi = cb[:, :, pl.ds(pl.multiple_of(3 * COL + t * 256, 256), 256)].reshape(TOK, 256)
            blk = jnp.where(keep, dot(a, lo), dot(a, hi)).astype(BF16)
            part[p, :, g, :, pl.ds(pl.multiple_of(t * 256, 256), 256)] = blk.reshape(4, 128, 256)
            return 0

        lax.fori_loop(0, 6, grad, 0)
        for dy in (2, 1, 3):
            post(*y_args(p, dy))

    for dy in range(1, 4):
        for zz in range(4):
            yy = (y + dy) % 4
            done(wp.at[:, yy, zz], w3_rs.at[yy * 4 + zz])

    def unpack(i, _):
        g, t = i // 3, i % 3
        rows = pl.ds(pl.multiple_of(g * NAT, NAT), NAT)
        rest = jnp.zeros((NAT, 256), F32)
        for p in range(3):
            blk = wp[g, :, :, :, pl.ds(pl.multiple_of(p * COL + t * 256, 256), 256)].reshape(ROWS, 256)
            wn[rows, pl.ds(pl.multiple_of(p * COL + t * 256, 256), 256)] = dot(um[0], blk).astype(BF16)
            rest += dot(um[p + 1], blk)
        wn[rows, pl.ds(pl.multiple_of(3 * COL + t * 256, 256), 256)] = rest.astype(BF16)
        return 0

    lax.fori_loop(0, 6, unpack, 0)

    def d_out(i, _):
        cols = pl.ds(pl.multiple_of(i * 256, 256), 256)
        dob[:, cols] = dot(cb[...].reshape(TOK, D), wn[cols, :], NT).astype(BF16)
        return 0

    lax.fori_loop(0, 3, d_out, 0)

    def backward(h, _):
        cols = pl.ds(pl.multiple_of(h * HDIM, HDIM), HDIM)
        do = dob[:, cols]
        pr = prob[h]
        gvb[:, :, cols] = dot(pr.astype(BF16), do, TN).astype(BF16).reshape(FRAMES, POS, HDIM)
        dpr = dot(do, head(vb, h), NT)
        ds = (pr * (dpr - jnp.sum(pr * dpr, axis=-1, keepdims=True))).astype(BF16)
        gqb[:, :, cols] = (dot(ds, head(kb, h)) * scale).astype(BF16).reshape(FRAMES, POS, HDIM)
        gkb[:, :, cols] = (dot(ds, head(qb, h), TN) * scale).astype(BF16).reshape(FRAMES, POS, HDIM)
        return 0

    lax.fori_loop(0, HEADS, backward, 0)

    def g_args(arr, dx, kz):
        px, pz = (x + dx) % 4, (zl + kz) % 2
        src = (gqb, gkb, gvb)[arr].at[pl.ds(pl.multiple_of((px * 2 + pz) * 4, 4), 4)]
        dst = (gq_out, gk_out, gv_out)[arr].at[
            :, pl.ds(pl.multiple_of(x * 16, 16), 16), pl.ds(pl.multiple_of(c * HALF, HALF), HALF)
        ]
        return src, dst, g_ss.at[arr, dx * 2 + kz], g_rs.at[arr, x * 2 + c], dev(px, y, zh * 2 + pz, zl)

    def g_each(fn):
        for arr in range(3):
            for dx in (2, 1, 3, 0):
                for kz in range(2):
                    fn(arr, dx, kz, a_own if dx == 0 and kz == 0 else None)

    g_each(lambda arr, dx, kz, own: post(*g_args(arr, dx, kz), own=own))

    def z_args(p, dz):
        to = (z + dz) % 4
        src = s1.at[p, :, pl.ds(pl.multiple_of(to * 32, 32), 32), :]
        return (src, rz.at[p, z], z_ss.at[p, dz - 1], z_rs.at[p, z], dev(x, y, to, c))

    for p in range(3):
        for dy in range(1, 4):
            yy = (y + dy) % 4
            done(ry.at[p, yy], y_rs.at[p, yy])
        total = part[p, y].astype(F32)
        for dy in range(1, 4):
            total += ry[p, (y + dy) % 4].astype(F32)
        s1[p] = total.astype(BF16)
        for dz in (2, 1, 3):
            post(*z_args(p, dz))

    def x_args(p, i, kc):
        core = (c + kc) % 2
        src = s2.at[p, i, pl.ds(pl.multiple_of(core * 16, 16), 16), :]
        return (src, rf.at[p, x], x_ss.at[p, i * 2 + kc], x_rs.at[p, x], dev(c * 2 + i, y, z, core))

    def x_own(i, kc):
        return x == c * 2 + i if kc == 0 else None

    for p in range(3):
        for dz in range(1, 4):
            zz = (z + dz) % 4
            done(rz.at[p, zz], z_rs.at[p, zz])
        total = s1[p, :, pl.ds(pl.multiple_of(z * 32, 32), 32), :].astype(F32)
        for dz in range(1, 4):
            total += rz[p, (z + dz) % 4].astype(F32)
        s2[p] = total.astype(BF16)
        for i in range(2):
            for kc in range(2):
                post(*x_args(p, i, kc), own=x_own(i, kc))

    norm = 1.0 / math.sqrt(32768.0)
    for p in range(3):
        for i in range(4):
            done(rf.at[p, i], x_rs.at[p, i])
        total = rf[p, 0].astype(F32)
        for i in range(1, 4):
            total += rf[p, i].astype(F32)
        gw_out[:, p * COL : (p + 1) * COL] = total * norm

    for arr in range(3):
        for i in range(8):
            col = pl.ds((i % 2) * HALF, HALF)
            done((gq_out, gk_out, gv_out)[arr].at[:, pl.ds((i // 2) * 16, 16), col], g_rs.at[arr, i])
    g_each(lambda arr, dx, kz, own: sent(g_args(arr, dx, kz)[0], g_ss.at[arr, dx * 2 + kz], own))
    a_each(lambda arr, dx, kc, own: sent(a_args(arr, dx, kc)[0], a_ss.at[arr, dx * 2 + kc], own))
    for dx in range(4):
        sent(w_in, w1_ss.at[dx], w_own if dx == 0 else None)
    for dz in range(1, 4):
        sent(w2_args(dz)[0], w2_ss.at[dz - 1])
    for dz in range(4):
        for dy in range(1, 4):
            sent(w3_args(dz, dy)[0], w3_ss.at[dz * 3 + dy - 1])
    for s in range(8):
        sent(cb.at[pl.ds(s * 4, 4), :, own_col], f_ss.at[s])
    for p in range(3):
        for d in range(1, 4):
            sent(y_args(p, d)[0], y_ss.at[p, d - 1])
            sent(z_args(p, d)[0], z_ss.at[p, d - 1])
        for i in range(2):
            for kc in range(2):
                sent(x_args(p, i, kc)[0], x_ss.at[p, i * 2 + kc], x_own(i, kc))


def local(query_in, key_in, value_in, cotangent, out_weight):
    top, rest = out_weight[:, :PK], out_weight[:, PK:]
    tail = rest.reshape(3, 4, COL).transpose(1, 0, 2).reshape(4, PK)
    w_packed = jnp.concatenate([top, tail], axis=0)
    any_spec = pl.BlockSpec(memory_space=pl.ANY)
    vmem_spec = pl.BlockSpec(memory_space=pltpu.VMEM)
    dma = pltpu.SemaphoreType.DMA
    act = jax.ShapeDtypeStruct((4, 64, HD), BF16)
    tok = (FRAMES, POS, HALF)
    gq, gk, gv, gw = pl.pallas_call(
        kernel,
        out_shape=(act, act, act, jax.ShapeDtypeStruct((16, PK), F32)),
        in_specs=[any_spec] * 4 + [vmem_spec],
        out_specs=(any_spec, any_spec, any_spec, vmem_spec),
        scratch_shapes=[
            pltpu.VMEM(tok, BF16), pltpu.VMEM(tok, BF16), pltpu.VMEM(tok, BF16),
            pltpu.VMEM((FRAMES, POS, D), BF16),
            pltpu.VMEM((2, 4, 4, 32, PK), BF16),
            pltpu.VMEM((HALF, D), BF16),
            pltpu.VMEM((HEADS, TOK, TOK), F32),
            pltpu.VMEM((TOK, HALF), BF16),
            pltpu.VMEM((3, 2, ROWS, TOK), BF16),
            pltpu.VMEM((3, ROWS, NAT), BF16),
            pltpu.VMEM((4, NAT, ROWS), BF16),
            pltpu.VMEM((3, 4, 2, 128, COL), BF16),
            pltpu.VMEM((3, 4, 2, 128, COL), BF16),
            pltpu.VMEM((3, 2, 128, COL), BF16),
            pltpu.VMEM((3, 4, 2, 32, COL), BF16),
            pltpu.VMEM((3, 2, 32, COL), BF16),
            pltpu.VMEM((3, 4, 16, COL), BF16),
            pltpu.VMEM((TOK, HALF), BF16),
            pltpu.VMEM(tok, BF16), pltpu.VMEM(tok, BF16), pltpu.VMEM(tok, BF16),
            dma((4, 8)), dma((4, 8)), dma((8,)), dma((8,)),
            dma((4,)), dma((4,)), dma((3,)), dma((4,)), dma((12,)), dma((16,)),
            dma((3, 3)), dma((3, 4)), dma((3, 3)), dma((3, 4)), dma((3, 4)), dma((3, 4)),
            dma((3, 8)), dma((3, 8)),
        ],
        compiler_params=pltpu.CompilerParams(
            collective_id=0, has_side_effects=True, vmem_limit_bytes=58 * 2**20
        ),
    )(
        query_in.reshape(4, 64, HD), key_in.reshape(4, 64, HD), value_in.reshape(4, 64, HD),
        cotangent.reshape(4, 64, D), w_packed,
    )
    tail = gw[12:].reshape(4, 3, COL).transpose(1, 0, 2).reshape(12, COL)
    grad_weight = jnp.concatenate([gw[:12], tail], axis=1)
    shape = (1, 4, 64, HD)
    return gq.reshape(shape), gk.reshape(shape), gv.reshape(shape), grad_weight


def solution(mesh):
    act, rows = P("dp", "seq", None, None), P(("seq", "dp"), None)
    return jax.shard_map(
        local, mesh=mesh, in_specs=(act, act, act, act, rows), out_specs=(act, act, act, rows),
        check_vma=False,
    )
```

```python
import math

import jax
import jax.numpy as jnp
from jax import lax
from jax.experimental import pallas as pl
from jax.experimental.pallas import tpu as pltpu
from jax.sharding import PartitionSpec as P

MESH = pl.DeviceIdType.MESH
F32, BF16 = jnp.float32, jnp.bfloat16

FRAMES, POS, HD, D, HDIM = 32, 16, 1536, 3072, 128
HALF = HD // 2
TOK = FRAMES * POS
HEADS = HALF // HDIM
PK = 2304
COL = 768
ROWS = 512
NAT = 384
NT = (((1,), (1,)), ((), ()))
TN = (((0,), (0,)), ((), ()))


def dot(a, b, dims=(((1,), (0,)), ((), ()))):
    return lax.dot_general(a, b, dims, preferred_element_type=F32)


def kernel(
    q_in, k_in, v_in, c_in, w_in,
    gq_out, gk_out, gv_out, gw_out,
    qb, kb, vb, cb, wf, wpk, wp, wn, prob, ao, aot, em, um, part, rh, ry, s1, rzh, rz, s2, rf, dob, gqb, gkb, gvb,
    a_ss, a_rs, f_ss, f_rs, w1_ss, w1_rs, w2_ss, w2_rs, w3_ss, w3_rs,
    y_ss, y_rs, z_ss, z_rs, x_ss, x_rs, g_ss, g_rs,
):
    seq, dp = lax.axis_index("seq"), lax.axis_index("dp")
    x, zl = seq // 2, seq % 2
    zh, y, c = dp // 8, (dp // 2) % 4, dp % 2
    z = zh * 2 + zl

    def dev(x, y, z, c):
        return {"seq": x * 2 + z % 2, "dp": (z // 2) * 8 + y * 2 + c}

    def remote(src, dst, ss, rs, to):
        return pltpu.make_async_remote_copy(
            src_ref=src, dst_ref=dst, send_sem=ss, recv_sem=rs, device_id=to, device_id_type=MESH
        )

    def done(ref, sem):
        pltpu.make_async_copy(ref, ref, sem).wait()

    def post(src, dst, ss, rs, to, own=None):
        if own is None:
            remote(src, dst, ss, rs, to).start()
            return

        @pl.when(own)
        def _():
            pltpu.make_async_copy(src, dst, rs).start()

        @pl.when(jnp.logical_not(own))
        def _():
            remote(src, dst, ss, rs, to).start()

    def sent(src, ss, own=None):
        if own is None:
            done(src, ss)
        else:
            pl.when(jnp.logical_not(own))(lambda: done(src, ss))

    z1, z3 = zh * 2 + 1 - zl, 3 - z
    z2 = (z + 2) % 4
    up, down = (y + 1) % 4, (y + 3) % 4
    far = (y + 2) % 4

    barrier = pltpu.get_barrier_semaphore()
    peers = [
        dev((x + dx) % 4, y, zh * 2 + (zl + kz) % 2, (c + kc) % 2)
        for dx in range(4) for kz in range(2) for kc in range(2) if dx or kz or kc
    ]
    peers += [dev(x, y, z3, c), dev(x, up, z, c), dev(x, down, z, c)]
    for to in peers:
        pl.semaphore_signal(barrier, inc=1, device_id=to, device_id_type=MESH)

    rows = w_in[...].astype(F32)
    wf[0:12, :] = rows[:, :PK]
    for p in range(3):
        wf[12:16, p * COL : (p + 1) * COL] = rows[4 * p : 4 * p + 4, PK:]
    wpk[...] = wf[...].astype(BF16)
    pl.semaphore_wait(barrier, len(peers))

    half = x // 2
    w_own = c == half
    w_slot = wp.at[x % 2, y, z, pl.ds(pl.multiple_of(c * 16, 16), 16), :]

    def w1_args(dx):
        return (wpk, w_slot, w1_ss.at[dx], w1_rs.at[(x % 2) * 2 + c], dev((x + dx) % 4, y, z, half))

    for dx in (2, 1, 3, 0):
        post(*w1_args(dx), own=w_own if dx == 0 else None)

    mine = pl.ds(pl.multiple_of(seq * 4, 4), 4)
    cross = zl != c

    def cot_cols(core, part_no):
        other = core if part_no == 0 else 1 - core
        return pl.ds(pl.multiple_of(core * HD + other * COL, COL), COL)

    def a_args(arr, dx, kc):
        px, core = (x + dx) % 4, (c + kc) % 2
        to = dev(px, y, zh * 2 + c, core)
        pos = pl.ds(pl.multiple_of(px * 16, 16), 16)
        if arr < 3:
            col = pl.ds(pl.multiple_of(core * HALF, HALF), HALF)
            src = (q_in, k_in, v_in)[arr].at[:, pos, col]
            dst = (qb, kb, vb)[arr].at[mine]
        else:
            col = cot_cols(core, arr - 3)
            src = c_in.at[:, pos, col]
            dst = cb.at[mine, :, col]
        return src, dst, a_ss.at[arr, dx * 2 + kc], a_rs.at[arr, seq], to

    def a_post(arrs, crossing):
        @pl.when(cross if crossing else jnp.logical_not(cross))
        def _():
            for arr in arrs:
                for dx in (2, 1, 3, 0):
                    for kc in range(2):
                        src, dst, ss, rs, to = a_args(arr, dx, kc)
                        if not crossing and dx == 0 and kc == 0:
                            pltpu.make_async_copy(src, dst, rs).start()
                        else:
                            remote(src, dst, ss, rs, to).start()

    a_post((0, 1, 2), False)

    def packed(shape, axis):
        m = lax.broadcasted_iota(jnp.int32, shape, axis)
        j, r = m >> 4, m & 15
        owner = ((j >> 1) & 1) * 16 + ((j >> 2) & 1) * 8 + (j >> 3) * 2 + (j & 1)
        return owner * 12, r

    base, r = packed((ROWS, NAT), 0)
    n = lax.broadcasted_iota(jnp.int32, (ROWS, NAT), 1)
    for p in range(3):
        hit = n == jnp.where(r < 12, base + r, base + (r - 12 + 4 * p))
        em[p] = jnp.where(hit, 1.0, 0.0).astype(BF16)
    base, r = packed((NAT, ROWS), 1)
    n = lax.broadcasted_iota(jnp.int32, (NAT, ROWS), 0)
    um[0] = jnp.where(n == jnp.where(r < 12, base + r, -1), 1.0, 0.0).astype(BF16)
    for p in range(3):
        hit = n == jnp.where(r < 12, -1, base + (r - 12 + 4 * p))
        um[p + 1] = jnp.where(hit, 1.0, 0.0).astype(BF16)

    w_z = (z, z3, z1, z2)

    def w2_args(i):
        blk = wp.at[:, y, z] if i < 2 else wp.at[:, y, z1]
        return (blk, blk, w2_ss.at[i], w2_rs.at[i], dev(x, y, z1 if i == 0 else z3, c))

    def w3_args(i, k):
        zz = w_z[i]
        blk = (wp.at[:, y, zz], wp.at[:, y, zz], wp.at[0, down, zz], wp.at[1, up, zz])[k]
        to = dev(x, down if k % 2 else up, z, c)
        return (blk, blk, w3_ss.at[i, k], w3_rs.at[i, k], to)

    def w3_post(i):
        post(*w3_args(i, 0))
        post(*w3_args(i, 1))

    def w3_relay(i):
        done(wp.at[:, down, w_z[i]], w3_rs.at[i, 0])
        post(*w3_args(i, 2))
        done(wp.at[:, up, w_z[i]], w3_rs.at[i, 1])
        post(*w3_args(i, 3))

    for i in range(4):
        done(wp.at[i // 2, y, z, pl.ds((i % 2) * 16, 16), :], w1_rs.at[i])
    post(*w2_args(0))
    post(*w2_args(1))
    w3_post(0)
    a_post((0,), True)
    done(wp.at[:, y, z3], w2_rs.at[1])
    w3_post(1)
    w3_relay(0)
    done(wp.at[:, y, z1], w2_rs.at[0])
    post(*w2_args(2))
    w3_post(2)
    a_post((1, 2), True)
    a_post((3,), False)
    w3_relay(1)
    done(wp.at[:, y, z2], w2_rs.at[2])
    w3_post(3)
    a_post((3,), True)
    a_post((4,), False)
    w3_relay(2)
    a_post((4,), True)
    w3_relay(3)

    for s in range(8):
        for arr, buf in enumerate((qb, kb, vb)):
            done(buf.at[pl.ds(s * 4, 4)], a_rs.at[arr, s])

    scale = 1.0 / math.sqrt(HDIM)

    def head(buf, h):
        return buf[:, :, pl.ds(pl.multiple_of(h * HDIM, HDIM), HDIM)].reshape(TOK, HDIM)

    def forward(h, _):
        score = dot(head(qb, h), head(kb, h), NT) * scale
        row = lax.broadcasted_iota(jnp.int32, (TOK, TOK), 0)
        col = lax.broadcasted_iota(jnp.int32, (TOK, TOK), 1)
        score = jnp.where(((row ^ col) & 15) == 0, score, -1e30)
        e = jnp.exp(score - jnp.max(score, axis=-1, keepdims=True))
        pr = e / jnp.sum(e, axis=-1, keepdims=True)
        prob[h] = pr
        out = dot(pr.astype(BF16), head(vb, h))
        ao[:, pl.ds(pl.multiple_of(h * HDIM, HDIM), HDIM)] = out.astype(BF16)
        return 0

    lax.fori_loop(0, HEADS, forward, 0)
    for g in range(2):
        for p in range(3):
            aot[p, g] = dot(em[p], ao[:, g * NAT : (g + 1) * NAT], NT).astype(BF16)

    for i in range(4):
        done(wp.at[0, far, w_z[i]], w3_rs.at[i, 2])
        done(wp.at[1, far, w_z[i]], w3_rs.at[i, 3])

    def unpack(i, _):
        g, t = i // 3, i % 3
        rows = pl.ds(pl.multiple_of(g * NAT, NAT), NAT)
        rest = jnp.zeros((NAT, 256), F32)
        for p in range(3):
            blk = wp[g, :, :, :, pl.ds(pl.multiple_of(p * COL + t * 256, 256), 256)].reshape(ROWS, 256)
            wn[rows, pl.ds(pl.multiple_of(p * COL + t * 256, 256), 256)] = dot(um[0], blk).astype(BF16)
            rest += dot(um[p + 1], blk)
        wn[rows, pl.ds(pl.multiple_of(3 * COL + t * 256, 256), 256)] = rest.astype(BF16)
        return 0

    lax.fori_loop(0, 6, unpack, 0)

    twin = dev(x, y, z, (c + 1) % 2)

    def pass_on(k):
        for s in range(8):
            blk = cb.at[pl.ds(s * 4, 4), :, cot_cols(c, k)]
            done(blk, a_rs.at[3 + k, s])
            post(blk, blk, f_ss.at[k, s], f_rs.at[k, s], twin)

    def passed(k):
        for s in range(8):
            done(cb.at[pl.ds(s * 4, 4), :, cot_cols(1 - c, k)], f_rs.at[k, s])

    def y_args(p, k):
        src, dst = (
            (part.at[p, far, 0], rh.at[p, 0]), (part.at[p, far, 1], rh.at[p, 1]),
            (part.at[p, up, 1], ry.at[p, 0, 1]), (part.at[p, down, 0], ry.at[p, 1, 0]),
            (part.at[p, up, 0], ry.at[p, 0, 0]), (part.at[p, down, 1], ry.at[p, 1, 1]),
        )[k]
        return (src, dst, y_ss.at[p, k], y_rs.at[p, k], dev(x, down if k % 2 else up, z, c))

    def y_relay(p):
        for k, (to, i) in enumerate(((up, 0), (down, 1))):
            done(rh.at[p, k], y_rs.at[p, k])
            part[p, to, i] = (part[p, to, i].astype(F32) + rh[p, k].astype(F32)).astype(BF16)
            post(*y_args(p, k + 4))

    pass_on(0)
    passed(0)

    keep = (lax.broadcasted_iota(jnp.int32, (ROWS, 256), 0) & 15) < 12
    for p in range(3):
        def grad(i, _, p=p):
            g, t = i // 3, i % 3
            a = aot[p, g]
            lo = cb[:, :, pl.ds(pl.multiple_of(p * COL + t * 256, 256), 256)].reshape(TOK, 256)
            hi = cb[:, :, pl.ds(pl.multiple_of(3 * COL + t * 256, 256), 256)].reshape(TOK, 256)
            blk = jnp.where(keep, dot(a, lo), dot(a, hi)).astype(BF16)
            part[p, :, g, :, pl.ds(pl.multiple_of(t * 256, 256), 256)] = blk.reshape(4, 128, 256)
            return 0

        lax.fori_loop(0, 6, grad, 0)
        for k in range(4):
            post(*y_args(p, k))
        if p == 0:
            pass_on(1)
            passed(1)

    def d_out(i, _):
        cols = pl.ds(pl.multiple_of(i * 256, 256), 256)
        dob[:, cols] = dot(cb[...].reshape(TOK, D), wn[cols, :], NT).astype(BF16)
        return 0

    lax.fori_loop(0, 3, d_out, 0)

    def backward(h, _):
        cols = pl.ds(pl.multiple_of(h * HDIM, HDIM), HDIM)
        do = dob[:, cols]
        pr = prob[h]
        gvb[:, :, cols] = dot(pr.astype(BF16), do, TN).astype(BF16).reshape(FRAMES, POS, HDIM)
        dpr = dot(do, head(vb, h), NT)
        ds = (pr * (dpr - jnp.sum(pr * dpr, axis=-1, keepdims=True))).astype(BF16)
        gqb[:, :, cols] = (dot(ds, head(kb, h)) * scale).astype(BF16).reshape(FRAMES, POS, HDIM)
        gkb[:, :, cols] = (dot(ds, head(qb, h), TN) * scale).astype(BF16).reshape(FRAMES, POS, HDIM)
        return 0

    y_relay(0)
    lax.fori_loop(0, HEADS, backward, 0)

    def g_args(arr, dx, kz):
        px, pz = (x + dx) % 4, (zl + kz) % 2
        src = (gqb, gkb, gvb)[arr].at[pl.ds(pl.multiple_of((px * 2 + pz) * 4, 4), 4)]
        dst = (gq_out, gk_out, gv_out)[arr].at[
            :, pl.ds(pl.multiple_of(x * 16, 16), 16), pl.ds(pl.multiple_of(c * HALF, HALF), HALF)
        ]
        return src, dst, g_ss.at[arr, dx * 2 + kz], g_rs.at[arr, x * 2 + c], dev(px, y, zh * 2 + pz, zl)

    a_own = zl == c

    def g_each(fn):
        for arr in range(3):
            for dx in (2, 1, 3, 0):
                for kz in (1, 0):
                    fn(arr, dx, kz, a_own if dx == 0 and kz == 0 else None)

    g_each(lambda arr, dx, kz, own: post(*g_args(arr, dx, kz), own=own))
    y_relay(1)
    y_relay(2)

    def s1_rows(zz):
        return pl.ds(pl.multiple_of(zz * 32, 32), 32)

    def z_args(p, k):
        src = s1.at[p, :, s1_rows((z2, z3, z1)[k]), :]
        dst = (rzh.at[p], rz.at[p, 0], rz.at[p, 1])[k]
        return (src, dst, z_ss.at[p, k], z_rs.at[p, k], dev(x, y, z1 if k == 2 else z3, c))

    def y_sum(p):
        total = part[p, y].astype(F32)
        for k, dst in ((2, ry.at[p, 0, 1]), (3, ry.at[p, 1, 0]), (4, ry.at[p, 0, 0]), (5, ry.at[p, 1, 1])):
            done(dst, y_rs.at[p, k])
        s1[p] = (total + ry[p, 0].astype(F32) + ry[p, 1].astype(F32)).astype(BF16)
        post(*z_args(p, 0))
        post(*z_args(p, 1))

    def z_relay(p):
        done(rzh.at[p], z_rs.at[p, 0])
        rows = s1_rows(z1)
        s1[p, :, rows, :] = (s1[p, :, rows, :].astype(F32) + rzh[p].astype(F32)).astype(BF16)
        post(*z_args(p, 2))

    def x_args(p, i, kc):
        core = (c + kc) % 2
        src = s2.at[p, i, pl.ds(pl.multiple_of(core * 16, 16), 16), :]
        return (src, rf.at[p, x], x_ss.at[p, i * 2 + kc], x_rs.at[p, x], dev(c * 2 + i, y, z, core))

    def x_own(i, kc):
        return x == c * 2 + i if kc == 0 else None

    def z_sum(p):
        for k in range(2):
            done(rz.at[p, k], z_rs.at[p, k + 1])
        total = s1[p, :, s1_rows(z), :].astype(F32)
        s2[p] = (total + rz[p, 0].astype(F32) + rz[p, 1].astype(F32)).astype(BF16)
        for i in range(2):
            for kc in range(2):
                post(*x_args(p, i, kc), own=x_own(i, kc))

    y_sum(0)
    y_sum(1)
    z_relay(0)
    y_sum(2)
    z_relay(1)
    z_sum(0)
    z_relay(2)
    z_sum(1)
    z_sum(2)

    norm = 1.0 / math.sqrt(32768.0)
    for p in range(3):
        for i in range(4):
            done(rf.at[p, i], x_rs.at[p, i])
        total = rf[p, 0].astype(F32)
        for i in range(1, 4):
            total += rf[p, i].astype(F32)
        total *= norm
        gw_out[:, p * COL : (p + 1) * COL] = total[:12]
        gw_out[4 * p : 4 * p + 4, PK:] = total[12:]

    for arr in range(3):
        for i in range(8):
            col = pl.ds((i % 2) * HALF, HALF)
            done((gq_out, gk_out, gv_out)[arr].at[:, pl.ds((i // 2) * 16, 16), col], g_rs.at[arr, i])
    g_each(lambda arr, dx, kz, own: sent(g_args(arr, dx, kz)[0], g_ss.at[arr, dx * 2 + kz], own))
    for arr in range(5):
        for dx in range(4):
            for kc in range(2):
                own = a_own if dx == 0 and kc == 0 else None
                sent(a_args(arr, dx, kc)[0], a_ss.at[arr, dx * 2 + kc], own)
    for dx in range(4):
        sent(wpk, w1_ss.at[dx], w_own if dx == 0 else None)
    for i in range(3):
        sent(w2_args(i)[0], w2_ss.at[i])
    for i in range(4):
        for k in range(4):
            sent(w3_args(i, k)[0], w3_ss.at[i, k])
    for k in range(2):
        for s in range(8):
            sent(cb.at[pl.ds(s * 4, 4), :, cot_cols(c, k)], f_ss.at[k, s])
    for p in range(3):
        for k in range(6):
            sent(y_args(p, k)[0], y_ss.at[p, k])
        for k in range(3):
            sent(z_args(p, k)[0], z_ss.at[p, k])
        for i in range(2):
            for kc in range(2):
                sent(x_args(p, i, kc)[0], x_ss.at[p, i * 2 + kc], x_own(i, kc))


def local(query_in, key_in, value_in, cotangent, out_weight):
    any_spec = pl.BlockSpec(memory_space=pl.ANY)
    vmem_spec = pl.BlockSpec(memory_space=pltpu.VMEM)
    dma = pltpu.SemaphoreType.DMA
    act = jax.ShapeDtypeStruct((4, 64, HD), BF16)
    tok = (FRAMES, POS, HALF)
    gq, gk, gv, gw = pl.pallas_call(
        kernel,
        out_shape=(act, act, act, jax.ShapeDtypeStruct((12, D), F32)),
        in_specs=[any_spec] * 4 + [vmem_spec],
        out_specs=(any_spec, any_spec, any_spec, vmem_spec),
        scratch_shapes=[
            pltpu.VMEM(tok, BF16), pltpu.VMEM(tok, BF16), pltpu.VMEM(tok, BF16),
            pltpu.VMEM((FRAMES, POS, D), BF16),
            pltpu.VMEM((16, PK), F32),
            pltpu.VMEM((16, PK), BF16),
            pltpu.VMEM((2, 4, 4, 32, PK), BF16),
            pltpu.VMEM((HALF, D), BF16),
            pltpu.VMEM((HEADS, TOK, TOK), F32),
            pltpu.VMEM((TOK, HALF), BF16),
            pltpu.VMEM((3, 2, ROWS, TOK), BF16),
            pltpu.VMEM((3, ROWS, NAT), BF16),
            pltpu.VMEM((4, NAT, ROWS), BF16),
            pltpu.VMEM((3, 4, 2, 128, COL), BF16),
            pltpu.VMEM((3, 2, 128, COL), BF16),
            pltpu.VMEM((3, 2, 2, 128, COL), BF16),
            pltpu.VMEM((3, 2, 128, COL), BF16),
            pltpu.VMEM((3, 2, 32, COL), BF16),
            pltpu.VMEM((3, 2, 2, 32, COL), BF16),
            pltpu.VMEM((3, 2, 32, COL), BF16),
            pltpu.VMEM((3, 4, 16, COL), BF16),
            pltpu.VMEM((TOK, HALF), BF16),
            pltpu.VMEM(tok, BF16), pltpu.VMEM(tok, BF16), pltpu.VMEM(tok, BF16),
            dma((5, 8)), dma((5, 8)), dma((2, 8)), dma((2, 8)),
            dma((4,)), dma((4,)), dma((3,)), dma((3,)), dma((4, 4)), dma((4, 4)),
            dma((3, 6)), dma((3, 6)), dma((3, 3)), dma((3, 3)), dma((3, 4)), dma((3, 4)),
            dma((3, 8)), dma((3, 8)),
        ],
        compiler_params=pltpu.CompilerParams(
            collective_id=0, has_side_effects=True, vmem_limit_bytes=58 * 2**20
        ),
    )(
        query_in.reshape(4, 64, HD), key_in.reshape(4, 64, HD), value_in.reshape(4, 64, HD),
        cotangent.reshape(4, 64, D), out_weight,
    )
    shape = (1, 4, 64, HD)
    return gq.reshape(shape), gk.reshape(shape), gv.reshape(shape), gw


def solution(mesh):
    act, rows = P("dp", "seq", None, None), P(("seq", "dp"), None)
    return jax.shard_map(
        local, mesh=mesh, in_specs=(act, act, act, act, rows), out_specs=(act, act, act, rows),
        check_vma=False,
    )
```

```python
import math

import jax
import jax.numpy as jnp
from jax import lax
from jax.experimental import pallas as pl
from jax.experimental.pallas import tpu as pltpu
from jax.sharding import PartitionSpec as P

MESH = pl.DeviceIdType.MESH
F32, BF16 = jnp.float32, jnp.bfloat16

FRAMES, POS, HD, D, HDIM = 32, 16, 1536, 3072, 128
HALF = HD // 2
TOK = FRAMES * POS
HEADS = HALF // HDIM
PK = 2304
COL = 768
ROWS = 512
NAT = 384
NT = (((1,), (1,)), ((), ()))
TN = (((0,), (0,)), ((), ()))


def dot(a, b, dims=(((1,), (0,)), ((), ()))):
    return lax.dot_general(a, b, dims, preferred_element_type=F32)


def kernel(
    q_in, k_in, v_in, c_in, w_in,
    gq_out, gk_out, gv_out, gw_out,
    qb, kb, vb, cb, wf, wpk, wp, wn, prob, ao, aot, em, um, part, rh, ry, s1, rzh, rz, s2, rf, dob, gqb, gkb, gvb,
    a_ss, a_rs, f_ss, f_rs, w1_ss, w1_rs, w2_ss, w2_rs, w3_ss, w3_rs,
    y_ss, y_rs, z_ss, z_rs, x_ss, x_rs, g_ss, g_rs,
):
    seq, dp = lax.axis_index("seq"), lax.axis_index("dp")
    x, zl = seq // 2, seq % 2
    zh, y, c = dp // 8, (dp // 2) % 4, dp % 2
    z = zh * 2 + zl

    def dev(x, y, z, c):
        return {"seq": x * 2 + z % 2, "dp": (z // 2) * 8 + y * 2 + c}

    def remote(src, dst, ss, rs, to):
        return pltpu.make_async_remote_copy(
            src_ref=src, dst_ref=dst, send_sem=ss, recv_sem=rs, device_id=to, device_id_type=MESH
        )

    def done(ref, sem):
        pltpu.make_async_copy(ref, ref, sem).wait()

    def post(src, dst, ss, rs, to, own=None):
        if own is None:
            remote(src, dst, ss, rs, to).start()
            return

        @pl.when(own)
        def _():
            pltpu.make_async_copy(src, dst, rs).start()

        @pl.when(jnp.logical_not(own))
        def _():
            remote(src, dst, ss, rs, to).start()

    def sent(src, ss, own=None):
        if own is None:
            done(src, ss)
        else:
            pl.when(jnp.logical_not(own))(lambda: done(src, ss))

    z1, z3 = zh * 2 + 1 - zl, 3 - z
    z2 = (z + 2) % 4
    up, down = (y + 1) % 4, (y + 3) % 4
    far = (y + 2) % 4

    barrier = pltpu.get_barrier_semaphore()
    peers = [
        dev((x + dx) % 4, y, zh * 2 + (zl + kz) % 2, (c + kc) % 2)
        for dx in range(4) for kz in range(2) for kc in range(2) if dx or kz or kc
    ]
    peers += [dev(x, y, z3, c), dev(x, up, z, c), dev(x, down, z, c)]
    for to in peers:
        pl.semaphore_signal(barrier, inc=1, device_id=to, device_id_type=MESH)

    rows = w_in[...].astype(F32)
    wf[0:12, :] = rows[:, :PK]
    for p in range(3):
        wf[12:16, p * COL : (p + 1) * COL] = rows[4 * p : 4 * p + 4, PK:]
    wpk[...] = wf[...].astype(BF16)
    pl.semaphore_wait(barrier, len(peers))

    half = x // 2
    w_own = c == half
    w_slot = wp.at[x % 2, y, z, pl.ds(pl.multiple_of(c * 16, 16), 16), :]

    def w1_args(dx):
        return (wpk, w_slot, w1_ss.at[dx], w1_rs.at[(x % 2) * 2 + c], dev((x + dx) % 4, y, z, half))

    for dx in (2, 1, 3, 0):
        post(*w1_args(dx), own=w_own if dx == 0 else None)

    mine = pl.ds(pl.multiple_of(seq * 4, 4), 4)
    cross = zl != c

    def cot_cols(core, part_no):
        other = core if part_no == 0 else 1 - core
        return pl.ds(pl.multiple_of(core * HD + other * COL, COL), COL)

    def a_args(arr, dx, kc):
        px, core = (x + dx) % 4, (c + kc) % 2
        to = dev(px, y, zh * 2 + c, core)
        pos = pl.ds(pl.multiple_of(px * 16, 16), 16)
        if arr < 2:
            col = cot_cols(core, arr)
            src = c_in.at[:, pos, col]
            dst = cb.at[mine, :, col]
        else:
            g, i = (arr - 2) // 3, (arr - 2) % 3
            col = pl.ds(pl.multiple_of(core * HALF + g * NAT, NAT), NAT)
            src = (q_in, k_in, v_in)[i].at[:, pos, col]
            dst = (qb, kb, vb)[i].at[mine, :, pl.ds(g * NAT, NAT)]
        return src, dst, a_ss.at[arr, dx * 2 + kc], a_rs.at[arr, seq], to

    def a_post(arrs, crossing):
        @pl.when(cross if crossing else jnp.logical_not(cross))
        def _():
            for arr in arrs:
                for dx in (2, 1, 3, 0):
                    for kc in range(2):
                        src, dst, ss, rs, to = a_args(arr, dx, kc)
                        if not crossing and dx == 0 and kc == 0:
                            pltpu.make_async_copy(src, dst, rs).start()
                        else:
                            remote(src, dst, ss, rs, to).start()

    def a_sent(arrs):
        for arr in arrs:
            for dx in (2, 1, 3, 0):
                for kc in range(2):
                    sent(a_args(arr, dx, kc)[0], a_ss.at[arr, dx * 2 + kc], zl == c if dx == 0 and kc == 0 else None)

    a_post((0, 1), False)

    def packed(shape, axis):
        m = lax.broadcasted_iota(jnp.int32, shape, axis)
        j, r = m >> 4, m & 15
        owner = ((j >> 1) & 1) * 16 + ((j >> 2) & 1) * 8 + (j >> 3) * 2 + (j & 1)
        return owner * 12, r

    base, r = packed((ROWS, NAT), 0)
    n = lax.broadcasted_iota(jnp.int32, (ROWS, NAT), 1)
    for p in range(3):
        hit = n == jnp.where(r < 12, base + r, base + (r - 12 + 4 * p))
        em[p] = jnp.where(hit, 1.0, 0.0).astype(BF16)
    base, r = packed((NAT, ROWS), 1)
    n = lax.broadcasted_iota(jnp.int32, (NAT, ROWS), 0)
    um[0] = jnp.where(n == jnp.where(r < 12, base + r, -1), 1.0, 0.0).astype(BF16)
    for p in range(3):
        hit = n == jnp.where(r < 12, -1, base + (r - 12 + 4 * p))
        um[p + 1] = jnp.where(hit, 1.0, 0.0).astype(BF16)

    w_z = (z, z3, z1, z2)

    def w2_args(i):
        blk = wp.at[:, y, z] if i < 2 else wp.at[:, y, z1]
        return (blk, blk, w2_ss.at[i], w2_rs.at[i], dev(x, y, z1 if i == 0 else z3, c))

    def w3_args(i, k):
        zz = w_z[i]
        blk = (wp.at[:, y, zz], wp.at[:, y, zz], wp.at[0, down, zz], wp.at[1, up, zz])[k]
        to = dev(x, down if k % 2 else up, z, c)
        return (blk, blk, w3_ss.at[i, k], w3_rs.at[i, k], to)

    def w3_post(i):
        post(*w3_args(i, 0))
        post(*w3_args(i, 1))

    def w3_relay(i):
        done(wp.at[:, down, w_z[i]], w3_rs.at[i, 0])
        post(*w3_args(i, 2))
        done(wp.at[:, up, w_z[i]], w3_rs.at[i, 1])
        post(*w3_args(i, 3))

    twin = dev(x, y, z, (c + 1) % 2)

    def pass_on(k):
        for s in range(8):
            blk = cb.at[pl.ds(s * 4, 4), :, cot_cols(c, k)]
            done(blk, a_rs.at[k, s])
            post(blk, blk, f_ss.at[k, s], f_rs.at[k, s], twin)

    def passed(k):
        for s in range(8):
            done(cb.at[pl.ds(s * 4, 4), :, cot_cols(1 - c, k)], f_rs.at[k, s])

    for i in range(4):
        done(wp.at[i // 2, y, z, pl.ds((i % 2) * 16, 16), :], w1_rs.at[i])
    post(*w2_args(0))
    post(*w2_args(1))
    w3_post(0)
    a_post((0,), True)
    done(wp.at[:, y, z3], w2_rs.at[1])
    w3_post(1)
    w3_relay(0)
    done(wp.at[:, y, z1], w2_rs.at[0])
    post(*w2_args(2))
    w3_post(2)
    a_post((1,), True)
    a_post((2, 3, 4), False)
    a_sent((0,))
    a_post((2, 3, 4), True)
    w3_relay(1)
    pass_on(0)
    done(wp.at[:, y, z2], w2_rs.at[2])
    w3_post(3)
    w3_relay(2)
    a_sent((2, 3, 4))
    a_post((5, 6, 7), False)
    a_post((5, 6, 7), True)
    pass_on(1)
    w3_relay(3)

    def attn_ready(g):
        for s in range(8):
            for i, buf in enumerate((qb, kb, vb)):
                done(buf.at[pl.ds(s * 4, 4), :, pl.ds(g * NAT, NAT)], a_rs.at[2 + 3 * g + i, s])

    scale = 1.0 / math.sqrt(HDIM)

    def head(buf, h):
        return buf[:, :, pl.ds(pl.multiple_of(h * HDIM, HDIM), HDIM)].reshape(TOK, HDIM)

    def forward(h, _):
        score = dot(head(qb, h), head(kb, h), NT) * scale
        row = lax.broadcasted_iota(jnp.int32, (TOK, TOK), 0)
        col = lax.broadcasted_iota(jnp.int32, (TOK, TOK), 1)
        score = jnp.where(((row ^ col) & 15) == 0, score, -1e30)
        e = jnp.exp(score - jnp.max(score, axis=-1, keepdims=True))
        pr = e / jnp.sum(e, axis=-1, keepdims=True)
        prob[h] = pr
        out = dot(pr.astype(BF16), head(vb, h))
        ao[:, pl.ds(pl.multiple_of(h * HDIM, HDIM), HDIM)] = out.astype(BF16)
        return 0

    def unpack(i, _):
        g, t = i // 3, i % 3
        rows = pl.ds(pl.multiple_of(g * NAT, NAT), NAT)
        rest = jnp.zeros((NAT, 256), F32)
        for p in range(3):
            blk = wp[g, :, :, :, pl.ds(pl.multiple_of(p * COL + t * 256, 256), 256)].reshape(ROWS, 256)
            wn[rows, pl.ds(pl.multiple_of(p * COL + t * 256, 256), 256)] = dot(um[0], blk).astype(BF16)
            rest += dot(um[p + 1], blk)
        wn[rows, pl.ds(pl.multiple_of(3 * COL + t * 256, 256), 256)] = rest.astype(BF16)
        return 0

    keep = (lax.broadcasted_iota(jnp.int32, (ROWS, 256), 0) & 15) < 12

    def grad(g, p):
        st = g * 3 + p

        def tile(t, _):
            a = aot[p, g]
            cols = pl.ds(pl.multiple_of(t * 256, 256), 256)
            lo = cb[:, :, pl.ds(pl.multiple_of(p * COL + t * 256, 256), 256)].reshape(TOK, 256)
            hi = cb[:, :, pl.ds(pl.multiple_of(3 * COL + t * 256, 256), 256)].reshape(TOK, 256)
            blk = jnp.where(keep, dot(a, lo), dot(a, hi)).astype(BF16)
            part[st, :, :, cols] = blk.reshape(4, 128, 256)
            return 0

        lax.fori_loop(0, 3, tile, 0)
        for k in range(4):
            post(*y_args(st, k))

    lo, hi = pl.ds(0, 64), pl.ds(64, 64)

    def y_args(st, k):
        src, dst = (
            (part.at[st, far, lo], rh.at[st, 0]), (part.at[st, far, hi], rh.at[st, 1]),
            (part.at[st, up, hi], ry.at[st, 0, hi]), (part.at[st, down, lo], ry.at[st, 1, lo]),
            (part.at[st, up, lo], ry.at[st, 0, lo]), (part.at[st, down, hi], ry.at[st, 1, hi]),
        )[k]
        return (src, dst, y_ss.at[st, k], y_rs.at[st, k], dev(x, down if k % 2 else up, z, c))

    def y_relay(st):
        for k, (to, rows) in enumerate(((up, lo), (down, hi))):
            done(rh.at[st, k], y_rs.at[st, k])
            part[st, to, rows] = (part[st, to, rows].astype(F32) + rh[st, k].astype(F32)).astype(BF16)
            post(*y_args(st, k + 4))

    def forward_group(g):
        attn_ready(g)
        lax.fori_loop(3 * g, 3 * g + 3, forward, 0)
        for p in range(3):
            aot[p, g] = dot(em[p], ao[:, g * NAT : (g + 1) * NAT], NT).astype(BF16)
        if g == 0:
            passed(0)
            passed(1)
        for p in range(3):
            grad(g, p)

    def d_out(i, _):
        cols = pl.ds(pl.multiple_of(i * 256, 256), 256)
        dob[:, cols] = dot(cb[...].reshape(TOK, D), wn[cols, :], NT).astype(BF16)
        return 0


    def backward(h, _):
        cols = pl.ds(pl.multiple_of(h * HDIM, HDIM), HDIM)
        do = dob[:, cols]
        pr = prob[h]
        gvb[:, :, cols] = dot(pr.astype(BF16), do, TN).astype(BF16).reshape(FRAMES, POS, HDIM)
        dpr = dot(do, head(vb, h), NT)
        ds = (pr * (dpr - jnp.sum(pr * dpr, axis=-1, keepdims=True))).astype(BF16)
        gqb[:, :, cols] = (dot(ds, head(kb, h)) * scale).astype(BF16).reshape(FRAMES, POS, HDIM)
        gkb[:, :, cols] = (dot(ds, head(qb, h), TN) * scale).astype(BF16).reshape(FRAMES, POS, HDIM)
        return 0

    def g_args(g, arr, dx, kz):
        px, pz = (x + dx) % 4, (zl + kz) % 2
        src = (gqb, gkb, gvb)[arr].at[pl.ds(pl.multiple_of((px * 2 + pz) * 4, 4), 4), :, pl.ds(g * NAT, NAT)]
        dst = (gq_out, gk_out, gv_out)[arr].at[
            :, pl.ds(pl.multiple_of(x * 16, 16), 16), pl.ds(pl.multiple_of(c * HALF + g * NAT, NAT), NAT)
        ]
        i = g * 3 + arr
        return src, dst, g_ss.at[i, dx * 2 + kz], g_rs.at[i, x * 2 + c], dev(px, y, zh * 2 + pz, zl)

    a_own = zl == c

    def g_each(g, fn):
        for arr in range(3):
            for dx in (2, 1, 3, 0):
                for kz in (1, 0):
                    fn(g, arr, dx, kz, a_own if dx == 0 and kz == 0 else None)

    def backward_group(g):
        lax.fori_loop(3 * g, 3 * g + 3, backward, 0)
        g_each(g, lambda g, arr, dx, kz, own: post(*g_args(g, arr, dx, kz), own=own))

    def s1_rows(zz):
        return pl.ds(pl.multiple_of(zz * 32, 32), 32)

    def z_args(st, k):
        src = s1.at[st, s1_rows((z2, z3, z1)[k]), :]
        dst = (rzh.at[st], rz.at[st, 0], rz.at[st, 1])[k]
        return (src, dst, z_ss.at[st, k], z_rs.at[st, k], dev(x, y, z1 if k == 2 else z3, c))

    def y_sum(st):
        for k in range(2, 6):
            done(y_args(st, k)[1], y_rs.at[st, k])
        total = part[st, y].astype(F32) + ry[st, 0].astype(F32) + ry[st, 1].astype(F32)
        s1[st] = total.astype(BF16)
        post(*z_args(st, 0))
        post(*z_args(st, 1))

    def z_relay(st):
        done(rzh.at[st], z_rs.at[st, 0])
        rows = s1_rows(z1)
        s1[st, rows, :] = (s1[st, rows, :].astype(F32) + rzh[st].astype(F32)).astype(BF16)
        post(*z_args(st, 2))

    def x_args(st, kc):
        g, p, core = st // 3, st % 3, (c + kc) % 2
        src = s2.at[st, pl.ds(pl.multiple_of(core * 16, 16), 16), :]
        return (src, rf.at[p, x], x_ss.at[st, kc], x_rs.at[p, x], dev(c * 2 + g, y, z, core))

    def x_own(st, kc):
        return x == c * 2 + st // 3 if kc == 0 else None

    def z_sum(st):
        for k in range(2):
            done(rz.at[st, k], z_rs.at[st, k + 1])
        total = s1[st, s1_rows(z), :].astype(F32)
        s2[st] = (total + rz[st, 0].astype(F32) + rz[st, 1].astype(F32)).astype(BF16)
        for kc in range(2):
            post(*x_args(st, kc), own=x_own(st, kc))

    forward_group(0)
    for i in range(4):
        done(wp.at[0, far, w_z[i]], w3_rs.at[i, 2])
        done(wp.at[1, far, w_z[i]], w3_rs.at[i, 3])
    lax.fori_loop(0, 6, unpack, 0)
    y_relay(0)
    y_relay(1)
    y_relay(2)
    lax.fori_loop(0, 3, d_out, 0)
    backward_group(0)
    forward_group(1)
    y_relay(3)
    y_sum(0)
    y_sum(1)
    y_sum(2)
    backward_group(1)
    y_relay(4)
    y_relay(5)
    for st in range(3):
        z_relay(st)
    for st in range(3):
        z_sum(st)
    y_sum(3)
    y_sum(4)
    z_relay(3)
    y_sum(5)
    z_relay(4)
    z_sum(3)
    z_relay(5)
    z_sum(4)
    z_sum(5)

    norm = 1.0 / math.sqrt(32768.0)
    for p in range(3):
        for i in range(4):
            done(rf.at[p, i], x_rs.at[p, i])
        total = rf[p, 0].astype(F32)
        for i in range(1, 4):
            total += rf[p, i].astype(F32)
        total *= norm
        gw_out[:, p * COL : (p + 1) * COL] = total[:12]
        gw_out[4 * p : 4 * p + 4, PK:] = total[12:]

    for g in range(2):
        for arr in range(3):
            for i in range(8):
                pos = pl.ds((i // 2) * 16, 16)
                col = pl.ds((i % 2) * HALF + g * NAT, NAT)
                done((gq_out, gk_out, gv_out)[arr].at[:, pos, col], g_rs.at[g * 3 + arr, i])
        g_each(g, lambda g, arr, dx, kz, own: sent(g_args(g, arr, dx, kz)[0], g_ss.at[g * 3 + arr, dx * 2 + kz], own))
    a_sent((1, 5, 6, 7))
    for dx in range(4):
        sent(wpk, w1_ss.at[dx], w_own if dx == 0 else None)
    for i in range(3):
        sent(w2_args(i)[0], w2_ss.at[i])
    for i in range(4):
        for k in range(4):
            sent(w3_args(i, k)[0], w3_ss.at[i, k])
    for k in range(2):
        for s in range(8):
            sent(cb.at[pl.ds(s * 4, 4), :, cot_cols(c, k)], f_ss.at[k, s])
    for st in range(6):
        for k in range(6):
            sent(y_args(st, k)[0], y_ss.at[st, k])
        for k in range(3):
            sent(z_args(st, k)[0], z_ss.at[st, k])
        for kc in range(2):
            sent(x_args(st, kc)[0], x_ss.at[st, kc], x_own(st, kc))


def local(query_in, key_in, value_in, cotangent, out_weight):
    any_spec = pl.BlockSpec(memory_space=pl.ANY)
    vmem_spec = pl.BlockSpec(memory_space=pltpu.VMEM)
    dma = pltpu.SemaphoreType.DMA
    act = jax.ShapeDtypeStruct((4, 64, HD), BF16)
    tok = (FRAMES, POS, HALF)
    gq, gk, gv, gw = pl.pallas_call(
        kernel,
        out_shape=(act, act, act, jax.ShapeDtypeStruct((12, D), F32)),
        in_specs=[any_spec] * 4 + [vmem_spec],
        out_specs=(any_spec, any_spec, any_spec, vmem_spec),
        scratch_shapes=[
            pltpu.VMEM(tok, BF16), pltpu.VMEM(tok, BF16), pltpu.VMEM(tok, BF16),
            pltpu.VMEM((FRAMES, POS, D), BF16),
            pltpu.VMEM((16, PK), F32),
            pltpu.VMEM((16, PK), BF16),
            pltpu.VMEM((2, 4, 4, 32, PK), BF16),
            pltpu.VMEM((HALF, D), BF16),
            pltpu.VMEM((HEADS, TOK, TOK), F32),
            pltpu.VMEM((TOK, HALF), BF16),
            pltpu.VMEM((3, 2, ROWS, TOK), BF16),
            pltpu.VMEM((3, ROWS, NAT), BF16),
            pltpu.VMEM((4, NAT, ROWS), BF16),
            pltpu.VMEM((6, 4, 128, COL), BF16),
            pltpu.VMEM((6, 2, 64, COL), BF16),
            pltpu.VMEM((6, 2, 128, COL), BF16),
            pltpu.VMEM((6, 128, COL), BF16),
            pltpu.VMEM((6, 32, COL), BF16),
            pltpu.VMEM((6, 2, 32, COL), BF16),
            pltpu.VMEM((6, 32, COL), BF16),
            pltpu.VMEM((3, 4, 16, COL), BF16),
            pltpu.VMEM((TOK, HALF), BF16),
            pltpu.VMEM(tok, BF16), pltpu.VMEM(tok, BF16), pltpu.VMEM(tok, BF16),
            dma((8, 8)), dma((8, 8)), dma((2, 8)), dma((2, 8)),
            dma((4,)), dma((4,)), dma((3,)), dma((3,)), dma((4, 4)), dma((4, 4)),
            dma((6, 6)), dma((6, 6)), dma((6, 3)), dma((6, 3)), dma((6, 2)), dma((3, 4)),
            dma((6, 8)), dma((6, 8)),
        ],
        compiler_params=pltpu.CompilerParams(
            collective_id=0, has_side_effects=True, vmem_limit_bytes=58 * 2**20
        ),
    )(
        query_in.reshape(4, 64, HD), key_in.reshape(4, 64, HD), value_in.reshape(4, 64, HD),
        cotangent.reshape(4, 64, D), out_weight,
    )
    shape = (1, 4, 64, HD)
    return gq.reshape(shape), gk.reshape(shape), gv.reshape(shape), gw


def solution(mesh):
    act, rows = P("dp", "seq", None, None), P(("seq", "dp"), None)
    return jax.shard_map(
        local, mesh=mesh, in_specs=(act, act, act, act, rows), out_specs=(act, act, act, rows),
        check_vma=False,
    )
```

```python
import math

import jax
import jax.numpy as jnp
from jax import lax
from jax.experimental import pallas as pl
from jax.experimental.pallas import tpu as pltpu
from jax.sharding import PartitionSpec as P

MESH = pl.DeviceIdType.MESH
F32, BF16 = jnp.float32, jnp.bfloat16

FRAMES, POS, HD, D, HDIM = 32, 16, 1536, 3072, 128
HALF = HD // 2
TOK = FRAMES * POS
HEADS = HALF // HDIM
PK = 2304
COL = 768
ROWS = 512
NAT = 384
NT = (((1,), (1,)), ((), ()))
TN = (((0,), (0,)), ((), ()))


def dot(a, b, dims=(((1,), (0,)), ((), ()))):
    return lax.dot_general(a, b, dims, preferred_element_type=F32)


def kernel(
    q_in, k_in, v_in, c_in, w_in,
    gq_out, gk_out, gv_out, gw_out,
    qb, kb, vb, cb, wf, wpk, wp, wn, prob, ao, aot, em, um, part, rh, ry, s1, rzh, rz, s2, rf, dob, gqb, gkb, gvb,
    a_ss, a_rs, f_ss, f_rs, w1_ss, w1_rs, w2_ss, w2_rs, w3_ss, w3_rs,
    y_ss, y_rs, z_ss, z_rs, x_ss, x_rs, g_ss, g_rs,
):
    seq, dp = lax.axis_index("seq"), lax.axis_index("dp")
    x, zl = seq // 2, seq % 2
    zh, y, c = dp // 8, (dp // 2) % 4, dp % 2
    z = zh * 2 + zl

    def dev(x, y, z, c):
        return {"seq": x * 2 + z % 2, "dp": (z // 2) * 8 + y * 2 + c}

    def remote(src, dst, ss, rs, to):
        return pltpu.make_async_remote_copy(
            src_ref=src, dst_ref=dst, send_sem=ss, recv_sem=rs, device_id=to, device_id_type=MESH
        )

    def done(ref, sem):
        pltpu.make_async_copy(ref, ref, sem).wait()

    def post(src, dst, ss, rs, to, own=None):
        if own is None:
            remote(src, dst, ss, rs, to).start()
            return

        @pl.when(own)
        def _():
            pltpu.make_async_copy(src, dst, rs).start()

        @pl.when(jnp.logical_not(own))
        def _():
            remote(src, dst, ss, rs, to).start()

    def sent(src, ss, own=None):
        if own is None:
            done(src, ss)
        else:
            pl.when(jnp.logical_not(own))(lambda: done(src, ss))

    z1, z3 = zh * 2 + 1 - zl, 3 - z
    z2 = (z + 2) % 4
    up, down = (y + 1) % 4, (y + 3) % 4
    far = (y + 2) % 4

    barrier = pltpu.get_barrier_semaphore()
    peers = [
        dev((x + dx) % 4, y, zh * 2 + (zl + kz) % 2, (c + kc) % 2)
        for dx in range(4) for kz in range(2) for kc in range(2) if dx or kz or kc
    ]
    peers += [dev(x, y, z3, c), dev(x, up, z, c), dev(x, down, z, c)]
    for to in peers:
        pl.semaphore_signal(barrier, inc=1, device_id=to, device_id_type=MESH)

    rows = w_in[...].astype(F32)
    wf[0:12, :] = rows[:, :PK]
    for p in range(3):
        wf[12:16, p * COL : (p + 1) * COL] = rows[4 * p : 4 * p + 4, PK:]
    wpk[...] = wf[...].astype(BF16)
    pl.semaphore_wait(barrier, len(peers))

    half = x // 2
    w_own = c == half
    w_slot = wp.at[x % 2, y, z, pl.ds(pl.multiple_of(c * 16, 16), 16), :]

    def w1_args(dx):
        return (wpk, w_slot, w1_ss.at[dx], w1_rs.at[(x % 2) * 2 + c], dev((x + dx) % 4, y, z, half))

    for dx in (2, 1, 3, 0):
        post(*w1_args(dx), own=w_own if dx == 0 else None)

    mine = pl.ds(pl.multiple_of(seq * 4, 4), 4)
    cross = zl != c

    def cot_cols(core, part_no):
        other = core if part_no == 0 else 1 - core
        return pl.ds(pl.multiple_of(core * HD + other * COL, COL), COL)

    def a_args(arr, dx, kc):
        px, core = (x + dx) % 4, (c + kc) % 2
        to = dev(px, y, zh * 2 + c, core)
        pos = pl.ds(pl.multiple_of(px * 16, 16), 16)
        if arr < 2:
            col = cot_cols(core, arr)
            src = c_in.at[:, pos, col]
            dst = cb.at[mine, :, col]
        else:
            g, i = (arr - 2) // 3, (arr - 2) % 3
            col = pl.ds(pl.multiple_of(core * HALF + g * NAT, NAT), NAT)
            src = (q_in, k_in, v_in)[i].at[:, pos, col]
            dst = (qb, kb, vb)[i].at[mine, :, pl.ds(g * NAT, NAT)]
        return src, dst, a_ss.at[arr, dx * 2 + kc], a_rs.at[arr, seq], to

    def a_post(arrs, crossing):
        @pl.when(cross if crossing else jnp.logical_not(cross))
        def _():
            for arr in arrs:
                for dx in (2, 1, 3, 0):
                    for kc in range(2):
                        src, dst, ss, rs, to = a_args(arr, dx, kc)
                        if not crossing and dx == 0 and kc == 0:
                            pltpu.make_async_copy(src, dst, rs).start()
                        else:
                            remote(src, dst, ss, rs, to).start()

    def a_sent(arrs):
        for arr in arrs:
            for dx in (2, 1, 3, 0):
                for kc in range(2):
                    sent(a_args(arr, dx, kc)[0], a_ss.at[arr, dx * 2 + kc], zl == c if dx == 0 and kc == 0 else None)

    a_post((0, 1), False)

    def packed(shape, axis):
        m = lax.broadcasted_iota(jnp.int32, shape, axis)
        j, r = m >> 4, m & 15
        owner = ((j >> 1) & 1) * 16 + ((j >> 2) & 1) * 8 + (j >> 3) * 2 + (j & 1)
        return owner * 12, r

    base, r = packed((ROWS, NAT), 0)
    n = lax.broadcasted_iota(jnp.int32, (ROWS, NAT), 1)
    for p in range(3):
        hit = n == jnp.where(r < 12, base + r, base + (r - 12 + 4 * p))
        em[p] = jnp.where(hit, 1.0, 0.0).astype(BF16)
    base, r = packed((NAT, ROWS), 1)
    n = lax.broadcasted_iota(jnp.int32, (NAT, ROWS), 0)
    um[0] = jnp.where(n == jnp.where(r < 12, base + r, -1), 1.0, 0.0).astype(BF16)
    for p in range(3):
        hit = n == jnp.where(r < 12, -1, base + (r - 12 + 4 * p))
        um[p + 1] = jnp.where(hit, 1.0, 0.0).astype(BF16)

    w_z = (z, z3, z1, z2)

    def w2_args(i):
        blk = wp.at[:, y, z] if i < 2 else wp.at[:, y, z1]
        return (blk, blk, w2_ss.at[i], w2_rs.at[i], dev(x, y, z1 if i == 0 else z3, c))

    def w3_args(i, k):
        zz = w_z[i]
        blk = (wp.at[:, y, zz], wp.at[:, y, zz], wp.at[0, down, zz], wp.at[1, up, zz])[k]
        to = dev(x, down if k % 2 else up, z, c)
        return (blk, blk, w3_ss.at[i, k], w3_rs.at[i, k], to)

    def w3_post(i):
        post(*w3_args(i, 0))
        post(*w3_args(i, 1))

    def w3_relay(i):
        done(wp.at[:, down, w_z[i]], w3_rs.at[i, 0])
        post(*w3_args(i, 2))
        done(wp.at[:, up, w_z[i]], w3_rs.at[i, 1])
        post(*w3_args(i, 3))

    twin = dev(x, y, z, (c + 1) % 2)

    def pass_on(k):
        for s in range(8):
            blk = cb.at[pl.ds(s * 4, 4), :, cot_cols(c, k)]
            done(blk, a_rs.at[k, s])
            post(blk, blk, f_ss.at[k, s], f_rs.at[k, s], twin)

    def passed(k):
        for s in range(8):
            done(cb.at[pl.ds(s * 4, 4), :, cot_cols(1 - c, k)], f_rs.at[k, s])

    for i in range(4):
        done(wp.at[i // 2, y, z, pl.ds((i % 2) * 16, 16), :], w1_rs.at[i])
    post(*w2_args(0))
    post(*w2_args(1))
    w3_post(0)
    a_post((0,), True)
    done(wp.at[:, y, z3], w2_rs.at[1])
    w3_post(1)
    w3_relay(0)
    done(wp.at[:, y, z1], w2_rs.at[0])
    post(*w2_args(2))
    w3_post(2)
    a_post((1,), True)
    a_post((2, 3, 4), False)
    a_sent((0,))
    a_post((2, 3, 4), True)
    w3_relay(1)
    pass_on(0)
    done(wp.at[:, y, z2], w2_rs.at[2])
    w3_post(3)
    w3_relay(2)
    w3_relay(3)
    a_sent((2, 3, 4))
    a_post((5, 6, 7), False)
    a_post((5, 6, 7), True)
    pass_on(1)

    def attn_ready(g):
        for s in range(8):
            for i, buf in enumerate((qb, kb, vb)):
                done(buf.at[pl.ds(s * 4, 4), :, pl.ds(g * NAT, NAT)], a_rs.at[2 + 3 * g + i, s])

    scale = 1.0 / math.sqrt(HDIM)

    def head(buf, h):
        return buf[:, :, pl.ds(pl.multiple_of(h * HDIM, HDIM), HDIM)].reshape(TOK, HDIM)

    def forward(h, _):
        score = dot(head(qb, h), head(kb, h), NT) * scale
        row = lax.broadcasted_iota(jnp.int32, (TOK, TOK), 0)
        col = lax.broadcasted_iota(jnp.int32, (TOK, TOK), 1)
        score = jnp.where(((row ^ col) & 15) == 0, score, -1e30)
        e = jnp.exp(score - jnp.max(score, axis=-1, keepdims=True))
        pr = e / jnp.sum(e, axis=-1, keepdims=True)
        prob[h] = pr
        out = dot(pr.astype(BF16), head(vb, h))
        ao[:, pl.ds(pl.multiple_of(h * HDIM, HDIM), HDIM)] = out.astype(BF16)
        return 0

    def unpack(i, _):
        g, t = i // 3, i % 3
        rows = pl.ds(pl.multiple_of(g * NAT, NAT), NAT)
        rest = jnp.zeros((NAT, 256), F32)
        for p in range(3):
            blk = wp[g, :, :, :, pl.ds(pl.multiple_of(p * COL + t * 256, 256), 256)].reshape(ROWS, 256)
            wn[rows, pl.ds(pl.multiple_of(p * COL + t * 256, 256), 256)] = dot(um[0], blk).astype(BF16)
            rest += dot(um[p + 1], blk)
        wn[rows, pl.ds(pl.multiple_of(3 * COL + t * 256, 256), 256)] = rest.astype(BF16)
        return 0

    keep = (lax.broadcasted_iota(jnp.int32, (ROWS, 256), 0) & 15) < 12

    def grad(g, p):
        st = g * 3 + p

        def tile(t, _):
            a = aot[p, g]
            cols = pl.ds(pl.multiple_of(t * 256, 256), 256)
            lo = cb[:, :, pl.ds(pl.multiple_of(p * COL + t * 256, 256), 256)].reshape(TOK, 256)
            hi = cb[:, :, pl.ds(pl.multiple_of(3 * COL + t * 256, 256), 256)].reshape(TOK, 256)
            blk = jnp.where(keep, dot(a, lo), dot(a, hi)).astype(BF16)
            part[st, :, :, cols] = blk.reshape(4, 128, 256)
            return 0

        lax.fori_loop(0, 3, tile, 0)
        for k in range(4):
            post(*y_args(st, k))

    lo, hi = pl.ds(0, 64), pl.ds(64, 64)

    def y_args(st, k):
        src, dst = (
            (part.at[st, far, lo], rh.at[st, 0]), (part.at[st, far, hi], rh.at[st, 1]),
            (part.at[st, up, hi], ry.at[st, 0, hi]), (part.at[st, down, lo], ry.at[st, 1, lo]),
            (part.at[st, up, lo], ry.at[st, 0, lo]), (part.at[st, down, hi], ry.at[st, 1, hi]),
        )[k]
        return (src, dst, y_ss.at[st, k], y_rs.at[st, k], dev(x, down if k % 2 else up, z, c))

    def y_relay(st):
        for k, (to, rows) in enumerate(((up, lo), (down, hi))):
            done(rh.at[st, k], y_rs.at[st, k])
            part[st, to, rows] = (part[st, to, rows].astype(F32) + rh[st, k].astype(F32)).astype(BF16)
            post(*y_args(st, k + 4))

    def forward_group(g):
        attn_ready(g)
        lax.fori_loop(3 * g, 3 * g + 3, forward, 0)
        for p in range(3):
            aot[p, g] = dot(em[p], ao[:, g * NAT : (g + 1) * NAT], NT).astype(BF16)
        if g == 0:
            passed(0)
            passed(1)
        for p in range(3):
            grad(g, p)

    def d_out(i, _):
        cols = pl.ds(pl.multiple_of(i * 256, 256), 256)
        dob[:, cols] = dot(cb[...].reshape(TOK, D), wn[cols, :], NT).astype(BF16)
        return 0


    def backward(h, _):
        cols = pl.ds(pl.multiple_of(h * HDIM, HDIM), HDIM)
        do = dob[:, cols]
        pr = prob[h]
        gvb[:, :, cols] = dot(pr.astype(BF16), do, TN).astype(BF16).reshape(FRAMES, POS, HDIM)
        dpr = dot(do, head(vb, h), NT)
        ds = (pr * (dpr - jnp.sum(pr * dpr, axis=-1, keepdims=True))).astype(BF16)
        gqb[:, :, cols] = (dot(ds, head(kb, h)) * scale).astype(BF16).reshape(FRAMES, POS, HDIM)
        gkb[:, :, cols] = (dot(ds, head(qb, h), TN) * scale).astype(BF16).reshape(FRAMES, POS, HDIM)
        return 0

    def g_args(g, arr, dx, kz):
        px, pz = (x + dx) % 4, (zl + kz) % 2
        src = (gqb, gkb, gvb)[arr].at[pl.ds(pl.multiple_of((px * 2 + pz) * 4, 4), 4), :, pl.ds(g * NAT, NAT)]
        dst = (gq_out, gk_out, gv_out)[arr].at[
            :, pl.ds(pl.multiple_of(x * 16, 16), 16), pl.ds(pl.multiple_of(c * HALF + g * NAT, NAT), NAT)
        ]
        i = g * 3 + arr
        return src, dst, g_ss.at[i, dx * 2 + kz], g_rs.at[i, x * 2 + c], dev(px, y, zh * 2 + pz, zl)

    a_own = zl == c

    def g_each(g, fn):
        for arr in range(3):
            for dx in (2, 1, 3, 0):
                for kz in (1, 0):
                    fn(g, arr, dx, kz, a_own if dx == 0 and kz == 0 else None)

    def backward_group(g):
        lax.fori_loop(3 * g, 3 * g + 3, backward, 0)
        g_each(g, lambda g, arr, dx, kz, own: post(*g_args(g, arr, dx, kz), own=own))

    def s1_rows(zz):
        return pl.ds(pl.multiple_of(zz * 32, 32), 32)

    def z_args(st, k):
        src = s1.at[st, s1_rows((z2, z3, z1)[k]), :]
        dst = (rzh.at[st], rz.at[st, 0], rz.at[st, 1])[k]
        return (src, dst, z_ss.at[st, k], z_rs.at[st, k], dev(x, y, z1 if k == 2 else z3, c))

    def y_sum(st):
        for k in range(2, 6):
            done(y_args(st, k)[1], y_rs.at[st, k])
        total = part[st, y].astype(F32) + ry[st, 0].astype(F32) + ry[st, 1].astype(F32)
        s1[st] = total.astype(BF16)
        post(*z_args(st, 0))
        post(*z_args(st, 1))

    def z_relay(st):
        done(rzh.at[st], z_rs.at[st, 0])
        rows = s1_rows(z1)
        s1[st, rows, :] = (s1[st, rows, :].astype(F32) + rzh[st].astype(F32)).astype(BF16)
        post(*z_args(st, 2))

    def x_args(st, kc):
        g, p, core = st // 3, st % 3, (c + kc) % 2
        src = s2.at[st, pl.ds(pl.multiple_of(core * 16, 16), 16), :]
        return (src, rf.at[p, x], x_ss.at[st, kc], x_rs.at[p, x], dev(c * 2 + g, y, z, core))

    def x_own(st, kc):
        return x == c * 2 + st // 3 if kc == 0 else None

    def z_sum(st):
        for k in range(2):
            done(rz.at[st, k], z_rs.at[st, k + 1])
        total = s1[st, s1_rows(z), :].astype(F32)
        s2[st] = (total + rz[st, 0].astype(F32) + rz[st, 1].astype(F32)).astype(BF16)
        for kc in range(2):
            post(*x_args(st, kc), own=x_own(st, kc))

    for i in range(4):
        done(wp.at[0, far, w_z[i]], w3_rs.at[i, 2])
        done(wp.at[1, far, w_z[i]], w3_rs.at[i, 3])
    lax.fori_loop(0, 6, unpack, 0)
    forward_group(0)
    lax.fori_loop(0, 3, d_out, 0)
    backward_group(0)
    y_relay(0)
    y_relay(1)
    y_relay(2)
    forward_group(1)
    y_relay(3)
    y_sum(0)
    y_sum(1)
    y_sum(2)
    backward_group(1)
    y_relay(4)
    y_relay(5)
    for st in range(3):
        z_relay(st)
    for st in range(3):
        z_sum(st)
    y_sum(3)
    y_sum(4)
    z_relay(3)
    y_sum(5)
    z_relay(4)
    z_sum(3)
    z_relay(5)
    z_sum(4)
    z_sum(5)

    norm = 1.0 / math.sqrt(32768.0)
    for p in range(3):
        for i in range(4):
            done(rf.at[p, i], x_rs.at[p, i])
        total = rf[p, 0].astype(F32)
        for i in range(1, 4):
            total += rf[p, i].astype(F32)
        total *= norm
        gw_out[:, p * COL : (p + 1) * COL] = total[:12]
        gw_out[4 * p : 4 * p + 4, PK:] = total[12:]

    for g in range(2):
        for arr in range(3):
            for i in range(8):
                pos = pl.ds((i // 2) * 16, 16)
                col = pl.ds((i % 2) * HALF + g * NAT, NAT)
                done((gq_out, gk_out, gv_out)[arr].at[:, pos, col], g_rs.at[g * 3 + arr, i])
        g_each(g, lambda g, arr, dx, kz, own: sent(g_args(g, arr, dx, kz)[0], g_ss.at[g * 3 + arr, dx * 2 + kz], own))
    a_sent((1, 5, 6, 7))
    for dx in range(4):
        sent(wpk, w1_ss.at[dx], w_own if dx == 0 else None)
    for i in range(3):
        sent(w2_args(i)[0], w2_ss.at[i])
    for i in range(4):
        for k in range(4):
            sent(w3_args(i, k)[0], w3_ss.at[i, k])
    for k in range(2):
        for s in range(8):
            sent(cb.at[pl.ds(s * 4, 4), :, cot_cols(c, k)], f_ss.at[k, s])
    for st in range(6):
        for k in range(6):
            sent(y_args(st, k)[0], y_ss.at[st, k])
        for k in range(3):
            sent(z_args(st, k)[0], z_ss.at[st, k])
        for kc in range(2):
            sent(x_args(st, kc)[0], x_ss.at[st, kc], x_own(st, kc))


def local(query_in, key_in, value_in, cotangent, out_weight):
    any_spec = pl.BlockSpec(memory_space=pl.ANY)
    vmem_spec = pl.BlockSpec(memory_space=pltpu.VMEM)
    dma = pltpu.SemaphoreType.DMA
    act = jax.ShapeDtypeStruct((4, 64, HD), BF16)
    tok = (FRAMES, POS, HALF)
    gq, gk, gv, gw = pl.pallas_call(
        kernel,
        out_shape=(act, act, act, jax.ShapeDtypeStruct((12, D), F32)),
        in_specs=[any_spec] * 4 + [vmem_spec],
        out_specs=(any_spec, any_spec, any_spec, vmem_spec),
        scratch_shapes=[
            pltpu.VMEM(tok, BF16), pltpu.VMEM(tok, BF16), pltpu.VMEM(tok, BF16),
            pltpu.VMEM((FRAMES, POS, D), BF16),
            pltpu.VMEM((16, PK), F32),
            pltpu.VMEM((16, PK), BF16),
            pltpu.VMEM((2, 4, 4, 32, PK), BF16),
            pltpu.VMEM((HALF, D), BF16),
            pltpu.VMEM((HEADS, TOK, TOK), F32),
            pltpu.VMEM((TOK, HALF), BF16),
            pltpu.VMEM((3, 2, ROWS, TOK), BF16),
            pltpu.VMEM((3, ROWS, NAT), BF16),
            pltpu.VMEM((4, NAT, ROWS), BF16),
            pltpu.VMEM((6, 4, 128, COL), BF16),
            pltpu.VMEM((6, 2, 64, COL), BF16),
            pltpu.VMEM((6, 2, 128, COL), BF16),
            pltpu.VMEM((6, 128, COL), BF16),
            pltpu.VMEM((6, 32, COL), BF16),
            pltpu.VMEM((6, 2, 32, COL), BF16),
            pltpu.VMEM((6, 32, COL), BF16),
            pltpu.VMEM((3, 4, 16, COL), BF16),
            pltpu.VMEM((TOK, HALF), BF16),
            pltpu.VMEM(tok, BF16), pltpu.VMEM(tok, BF16), pltpu.VMEM(tok, BF16),
            dma((8, 8)), dma((8, 8)), dma((2, 8)), dma((2, 8)),
            dma((4,)), dma((4,)), dma((3,)), dma((3,)), dma((4, 4)), dma((4, 4)),
            dma((6, 6)), dma((6, 6)), dma((6, 3)), dma((6, 3)), dma((6, 2)), dma((3, 4)),
            dma((6, 8)), dma((6, 8)),
        ],
        compiler_params=pltpu.CompilerParams(
            collective_id=0, has_side_effects=True, vmem_limit_bytes=58 * 2**20
        ),
    )(
        query_in.reshape(4, 64, HD), key_in.reshape(4, 64, HD), value_in.reshape(4, 64, HD),
        cotangent.reshape(4, 64, D), out_weight,
    )
    shape = (1, 4, 64, HD)
    return gq.reshape(shape), gk.reshape(shape), gv.reshape(shape), gw


def solution(mesh):
    act, rows = P("dp", "seq", None, None), P(("seq", "dp"), None)
    return jax.shard_map(
        local, mesh=mesh, in_specs=(act, act, act, act, rows), out_specs=(act, act, act, rows),
        check_vma=False,
    )
```

```python
import math

import jax
import jax.numpy as jnp
from jax import lax
from jax.experimental import pallas as pl
from jax.experimental.pallas import tpu as pltpu
from jax.sharding import PartitionSpec as P

MESH = pl.DeviceIdType.MESH
F32, BF16 = jnp.float32, jnp.bfloat16

FRAMES, POS, HD, D, HDIM = 32, 16, 1536, 3072, 128
HALF = HD // 2
TOK = FRAMES * POS
HEADS = HALF // HDIM
PK = 2304
COL = 768
ROWS = 512
NAT = 384
NT = (((1,), (1,)), ((), ()))
TN = (((0,), (0,)), ((), ()))


def dot(a, b, dims=(((1,), (0,)), ((), ()))):
    return lax.dot_general(a, b, dims, preferred_element_type=F32)


def kernel(
    q_in, k_in, v_in, c_in, w_in,
    gq_out, gk_out, gv_out, gw_out,
    qb, kb, vb, cb, wf, wpk, wp, wn, prob, ao, aot, em, um, part, rh, ry, s1, rzh, rz, s2, rf, dob, gqb, gkb, gvb,
    a_ss, a_rs, f_ss, f_rs, w1_ss, w1_rs, w2_ss, w2_rs, w3_ss, w3_rs,
    y_ss, y_rs, z_ss, z_rs, x_ss, x_rs, g_ss, g_rs,
):
    seq, dp = lax.axis_index("seq"), lax.axis_index("dp")
    x, zl = seq // 2, seq % 2
    zh, y, c = dp // 8, (dp // 2) % 4, dp % 2
    z = zh * 2 + zl

    def dev(x, y, z, c):
        return {"seq": x * 2 + z % 2, "dp": (z // 2) * 8 + y * 2 + c}

    def remote(src, dst, ss, rs, to):
        return pltpu.make_async_remote_copy(
            src_ref=src, dst_ref=dst, send_sem=ss, recv_sem=rs, device_id=to, device_id_type=MESH
        )

    def done(ref, sem):
        pltpu.make_async_copy(ref, ref, sem).wait()

    def post(src, dst, ss, rs, to, own=None):
        if own is None:
            remote(src, dst, ss, rs, to).start()
            return

        @pl.when(own)
        def _():
            pltpu.make_async_copy(src, dst, rs).start()

        @pl.when(jnp.logical_not(own))
        def _():
            remote(src, dst, ss, rs, to).start()

    def sent(src, ss, own=None):
        if own is None:
            done(src, ss)
        else:
            pl.when(jnp.logical_not(own))(lambda: done(src, ss))

    z1, z3 = zh * 2 + 1 - zl, 3 - z
    z2 = (z + 2) % 4
    up, down = (y + 1) % 4, (y + 3) % 4
    far = (y + 2) % 4

    barrier = pltpu.get_barrier_semaphore()
    peers = [
        dev((x + dx) % 4, y, zh * 2 + (zl + kz) % 2, (c + kc) % 2)
        for dx in range(4) for kz in range(2) for kc in range(2) if dx or kz or kc
    ]
    peers += [dev(x, y, z3, c), dev(x, up, z, c), dev(x, down, z, c)]
    for to in peers:
        pl.semaphore_signal(barrier, inc=1, device_id=to, device_id_type=MESH)

    rows = w_in[...].astype(F32)
    wf[0:12, :] = rows[:, :PK]
    for p in range(3):
        wf[12:16, p * COL : (p + 1) * COL] = rows[4 * p : 4 * p + 4, PK:]
    wpk[...] = wf[...].astype(BF16)
    pl.semaphore_wait(barrier, len(peers))

    half = x // 2
    w_own = c == half
    w_slot = wp.at[x % 2, y, z, pl.ds(pl.multiple_of(c * 16, 16), 16), :]

    def w1_args(dx):
        return (wpk, w_slot, w1_ss.at[dx], w1_rs.at[(x % 2) * 2 + c], dev((x + dx) % 4, y, z, half))

    for dx in (2, 1, 3, 0):
        post(*w1_args(dx), own=w_own if dx == 0 else None)

    mine = pl.ds(pl.multiple_of(seq * 4, 4), 4)
    cross = zl != c

    def cot_cols(core, part_no):
        other = core if part_no == 0 else 1 - core
        return pl.ds(pl.multiple_of(core * HD + other * COL, COL), COL)

    def a_args(arr, dx, kc):
        px, core = (x + dx) % 4, (c + kc) % 2
        to = dev(px, y, zh * 2 + c, core)
        pos = pl.ds(pl.multiple_of(px * 16, 16), 16)
        if arr < 2:
            col = cot_cols(core, arr)
            src = c_in.at[:, pos, col]
            dst = cb.at[mine, :, col]
        else:
            g, i = (arr - 2) // 3, (arr - 2) % 3
            col = pl.ds(pl.multiple_of(core * HALF + g * NAT, NAT), NAT)
            src = (q_in, k_in, v_in)[i].at[:, pos, col]
            dst = (qb, kb, vb)[i].at[mine, :, pl.ds(g * NAT, NAT)]
        return src, dst, a_ss.at[arr, dx * 2 + kc], a_rs.at[arr, seq], to

    def a_post(arrs, crossing):
        @pl.when(cross if crossing else jnp.logical_not(cross))
        def _():
            for arr in arrs:
                for dx in (2, 1, 3, 0):
                    for kc in range(2):
                        src, dst, ss, rs, to = a_args(arr, dx, kc)
                        if not crossing and dx == 0 and kc == 0:
                            pltpu.make_async_copy(src, dst, rs).start()
                        else:
                            remote(src, dst, ss, rs, to).start()

    def a_sent(arrs):
        for arr in arrs:
            for dx in (2, 1, 3, 0):
                for kc in range(2):
                    sent(a_args(arr, dx, kc)[0], a_ss.at[arr, dx * 2 + kc], zl == c if dx == 0 and kc == 0 else None)

    a_post((0, 1), False)

    def packed(shape, axis):
        m = lax.broadcasted_iota(jnp.int32, shape, axis)
        j, r = m >> 4, m & 15
        owner = ((j >> 1) & 1) * 16 + ((j >> 2) & 1) * 8 + (j >> 3) * 2 + (j & 1)
        return owner * 12, r

    base, r = packed((ROWS, NAT), 0)
    n = lax.broadcasted_iota(jnp.int32, (ROWS, NAT), 1)
    for p in range(3):
        hit = n == jnp.where(r < 12, base + r, base + (r - 12 + 4 * p))
        em[p] = jnp.where(hit, 1.0, 0.0).astype(BF16)
    base, r = packed((NAT, ROWS), 1)
    n = lax.broadcasted_iota(jnp.int32, (NAT, ROWS), 0)
    um[0] = jnp.where(n == jnp.where(r < 12, base + r, -1), 1.0, 0.0).astype(BF16)
    for p in range(3):
        hit = n == jnp.where(r < 12, -1, base + (r - 12 + 4 * p))
        um[p + 1] = jnp.where(hit, 1.0, 0.0).astype(BF16)

    w_z = (z, z3, z1, z2)

    def w2_args(i):
        blk = wp.at[:, y, z] if i < 2 else wp.at[:, y, z1]
        return (blk, blk, w2_ss.at[i], w2_rs.at[i], dev(x, y, z1 if i == 0 else z3, c))

    def w3_args(i, k):
        zz = w_z[i]
        blk = (wp.at[:, y, zz], wp.at[:, y, zz], wp.at[0, down, zz], wp.at[1, up, zz])[k]
        to = dev(x, down if k % 2 else up, z, c)
        return (blk, blk, w3_ss.at[i, k], w3_rs.at[i, k], to)

    def w3_post(i):
        post(*w3_args(i, 0))
        post(*w3_args(i, 1))

    def w3_relay(i):
        done(wp.at[:, down, w_z[i]], w3_rs.at[i, 0])
        post(*w3_args(i, 2))
        done(wp.at[:, up, w_z[i]], w3_rs.at[i, 1])
        post(*w3_args(i, 3))

    twin = dev(x, y, z, (c + 1) % 2)

    def pass_on(k):
        for s in range(8):
            blk = cb.at[pl.ds(s * 4, 4), :, cot_cols(c, k)]
            done(blk, a_rs.at[k, s])
            post(blk, blk, f_ss.at[k, s], f_rs.at[k, s], twin)

    def passed(k):
        for s in range(8):
            done(cb.at[pl.ds(s * 4, 4), :, cot_cols(1 - c, k)], f_rs.at[k, s])

    for i in range(4):
        done(wp.at[i // 2, y, z, pl.ds((i % 2) * 16, 16), :], w1_rs.at[i])
    post(*w2_args(0))
    post(*w2_args(1))
    w3_post(0)
    a_post((0,), True)
    done(wp.at[:, y, z3], w2_rs.at[1])
    w3_post(1)
    w3_relay(0)
    done(wp.at[:, y, z1], w2_rs.at[0])
    post(*w2_args(2))
    w3_post(2)
    a_post((1,), True)
    a_post((2, 3, 4), False)
    a_sent((0,))
    a_post((2, 3, 4), True)
    w3_relay(1)
    pass_on(0)
    done(wp.at[:, y, z2], w2_rs.at[2])
    w3_post(3)
    w3_relay(2)
    w3_relay(3)
    a_sent((2, 3, 4))
    a_post((5, 6, 7), False)
    a_post((5, 6, 7), True)
    pass_on(1)

    def attn_ready(g):
        for s in range(8):
            for i, buf in enumerate((qb, kb, vb)):
                done(buf.at[pl.ds(s * 4, 4), :, pl.ds(g * NAT, NAT)], a_rs.at[2 + 3 * g + i, s])

    scale = 1.0 / math.sqrt(HDIM)

    def head(buf, h):
        return buf[:, :, pl.ds(pl.multiple_of(h * HDIM, HDIM), HDIM)].reshape(TOK, HDIM)

    def forward(h, _):
        score = dot(head(qb, h), head(kb, h), NT) * scale
        row = lax.broadcasted_iota(jnp.int32, (TOK, TOK), 0)
        col = lax.broadcasted_iota(jnp.int32, (TOK, TOK), 1)
        score = jnp.where(((row ^ col) & 15) == 0, score, -1e30)
        e = jnp.exp(score - jnp.max(score, axis=-1, keepdims=True))
        pr = e / jnp.sum(e, axis=-1, keepdims=True)
        prob[h] = pr
        out = dot(pr.astype(BF16), head(vb, h))
        ao[:, pl.ds(pl.multiple_of(h * HDIM, HDIM), HDIM)] = out.astype(BF16)
        return 0

    def unpack(i, _):
        g, t = i // 3, i % 3
        rows = pl.ds(pl.multiple_of(g * NAT, NAT), NAT)
        rest = jnp.zeros((NAT, 256), F32)
        for p in range(3):
            blk = wp[g, :, :, :, pl.ds(pl.multiple_of(p * COL + t * 256, 256), 256)].reshape(ROWS, 256)
            wn[rows, pl.ds(pl.multiple_of(p * COL + t * 256, 256), 256)] = dot(um[0], blk).astype(BF16)
            rest += dot(um[p + 1], blk)
        wn[rows, pl.ds(pl.multiple_of(3 * COL + t * 256, 256), 256)] = rest.astype(BF16)
        return 0

    keep = (lax.broadcasted_iota(jnp.int32, (ROWS, 256), 0) & 15) < 12

    def grad(g, p):
        st = g * 3 + p

        def tile(t, _):
            a = aot[p, g]
            cols = pl.ds(pl.multiple_of(t * 256, 256), 256)
            lo = cb[:, :, pl.ds(pl.multiple_of(p * COL + t * 256, 256), 256)].reshape(TOK, 256)
            hi = cb[:, :, pl.ds(pl.multiple_of(3 * COL + t * 256, 256), 256)].reshape(TOK, 256)
            blk = jnp.where(keep, dot(a, lo), dot(a, hi)).astype(BF16)
            part[st, :, :, cols] = blk.reshape(4, 128, 256)
            return 0

        lax.fori_loop(0, 3, tile, 0)
        for k in range(4):
            post(*y_args(st, k))

    lo, hi = pl.ds(0, 64), pl.ds(64, 64)

    def y_args(st, k):
        src, dst = (
            (part.at[st, far, lo], rh.at[st, 0]), (part.at[st, far, hi], rh.at[st, 1]),
            (part.at[st, up, hi], ry.at[st, 0, hi]), (part.at[st, down, lo], ry.at[st, 1, lo]),
            (part.at[st, up, lo], ry.at[st, 0, lo]), (part.at[st, down, hi], ry.at[st, 1, hi]),
        )[k]
        return (src, dst, y_ss.at[st, k], y_rs.at[st, k], dev(x, down if k % 2 else up, z, c))

    def y_relay(st):
        for k, (to, rows) in enumerate(((up, lo), (down, hi))):
            done(rh.at[st, k], y_rs.at[st, k])
            part[st, to, rows] = (part[st, to, rows].astype(F32) + rh[st, k].astype(F32)).astype(BF16)
            post(*y_args(st, k + 4))

    def forward_group(g):
        attn_ready(g)
        lax.fori_loop(3 * g, 3 * g + 3, forward, 0)
        for p in range(3):
            aot[p, g] = dot(em[p], ao[:, g * NAT : (g + 1) * NAT], NT).astype(BF16)
        if g == 0:
            passed(0)
            passed(1)
        else:
            backward_group(1)
        for p in range(3):
            grad(g, p)

    def d_out(i, _):
        cols = pl.ds(pl.multiple_of(i * 256, 256), 256)
        dob[:, cols] = dot(cb[...].reshape(TOK, D), wn[cols, :], NT).astype(BF16)
        return 0


    def backward(h, _):
        cols = pl.ds(pl.multiple_of(h * HDIM, HDIM), HDIM)
        do = dob[:, cols]
        pr = prob[h]
        gvb[:, :, cols] = dot(pr.astype(BF16), do, TN).astype(BF16).reshape(FRAMES, POS, HDIM)
        dpr = dot(do, head(vb, h), NT)
        ds = (pr * (dpr - jnp.sum(pr * dpr, axis=-1, keepdims=True))).astype(BF16)
        gqb[:, :, cols] = (dot(ds, head(kb, h)) * scale).astype(BF16).reshape(FRAMES, POS, HDIM)
        gkb[:, :, cols] = (dot(ds, head(qb, h), TN) * scale).astype(BF16).reshape(FRAMES, POS, HDIM)
        return 0

    def g_args(g, arr, dx, kz):
        px, pz = (x + dx) % 4, (zl + kz) % 2
        src = (gqb, gkb, gvb)[arr].at[pl.ds(pl.multiple_of((px * 2 + pz) * 4, 4), 4), :, pl.ds(g * NAT, NAT)]
        dst = (gq_out, gk_out, gv_out)[arr].at[
            :, pl.ds(pl.multiple_of(x * 16, 16), 16), pl.ds(pl.multiple_of(c * HALF + g * NAT, NAT), NAT)
        ]
        i = g * 3 + arr
        return src, dst, g_ss.at[i, dx * 2 + kz], g_rs.at[i, x * 2 + c], dev(px, y, zh * 2 + pz, zl)

    a_own = zl == c

    def g_each(g, fn):
        for arr in range(3):
            for dx in (2, 1, 3, 0):
                for kz in (1, 0):
                    fn(g, arr, dx, kz, a_own if dx == 0 and kz == 0 else None)

    def backward_group(g):
        lax.fori_loop(3 * g, 3 * g + 3, backward, 0)
        g_each(g, lambda g, arr, dx, kz, own: post(*g_args(g, arr, dx, kz), own=own))

    def s1_rows(zz):
        return pl.ds(pl.multiple_of(zz * 32, 32), 32)

    def z_args(st, k):
        src = s1.at[st, s1_rows((z2, z3, z1)[k]), :]
        dst = (rzh.at[st], rz.at[st, 0], rz.at[st, 1])[k]
        return (src, dst, z_ss.at[st, k], z_rs.at[st, k], dev(x, y, z1 if k == 2 else z3, c))

    def y_sum(st):
        for k in range(2, 6):
            done(y_args(st, k)[1], y_rs.at[st, k])
        total = part[st, y].astype(F32) + ry[st, 0].astype(F32) + ry[st, 1].astype(F32)
        s1[st] = total.astype(BF16)
        post(*z_args(st, 0))
        post(*z_args(st, 1))

    def z_relay(st):
        done(rzh.at[st], z_rs.at[st, 0])
        rows = s1_rows(z1)
        s1[st, rows, :] = (s1[st, rows, :].astype(F32) + rzh[st].astype(F32)).astype(BF16)
        post(*z_args(st, 2))

    def x_args(st, kc):
        g, p, core = st // 3, st % 3, (c + kc) % 2
        src = s2.at[st, pl.ds(pl.multiple_of(core * 16, 16), 16), :]
        return (src, rf.at[p, x], x_ss.at[st, kc], x_rs.at[p, x], dev(c * 2 + g, y, z, core))

    def x_own(st, kc):
        return x == c * 2 + st // 3 if kc == 0 else None

    def z_sum(st):
        for k in range(2):
            done(rz.at[st, k], z_rs.at[st, k + 1])
        total = s1[st, s1_rows(z), :].astype(F32)
        s2[st] = (total + rz[st, 0].astype(F32) + rz[st, 1].astype(F32)).astype(BF16)
        for kc in range(2):
            post(*x_args(st, kc), own=x_own(st, kc))

    for i in range(4):
        done(wp.at[0, far, w_z[i]], w3_rs.at[i, 2])
        done(wp.at[1, far, w_z[i]], w3_rs.at[i, 3])
    lax.fori_loop(0, 6, unpack, 0)
    forward_group(0)
    lax.fori_loop(0, 3, d_out, 0)
    backward_group(0)
    y_relay(0)
    y_relay(1)
    y_relay(2)
    forward_group(1)
    y_relay(3)
    y_sum(0)
    y_sum(1)
    y_sum(2)
    y_relay(4)
    y_relay(5)
    for st in range(3):
        z_relay(st)
    for st in range(3):
        z_sum(st)
    y_sum(3)
    y_sum(4)
    z_relay(3)
    y_sum(5)
    z_relay(4)
    z_sum(3)
    z_relay(5)
    z_sum(4)
    z_sum(5)

    norm = 1.0 / math.sqrt(32768.0)
    for p in range(3):
        for i in range(4):
            done(rf.at[p, i], x_rs.at[p, i])
        total = rf[p, 0].astype(F32)
        for i in range(1, 4):
            total += rf[p, i].astype(F32)
        total *= norm
        gw_out[:, p * COL : (p + 1) * COL] = total[:12]
        gw_out[4 * p : 4 * p + 4, PK:] = total[12:]

    for g in range(2):
        for arr in range(3):
            for i in range(8):
                pos = pl.ds((i // 2) * 16, 16)
                col = pl.ds((i % 2) * HALF + g * NAT, NAT)
                done((gq_out, gk_out, gv_out)[arr].at[:, pos, col], g_rs.at[g * 3 + arr, i])
        g_each(g, lambda g, arr, dx, kz, own: sent(g_args(g, arr, dx, kz)[0], g_ss.at[g * 3 + arr, dx * 2 + kz], own))
    a_sent((1, 5, 6, 7))
    for dx in range(4):
        sent(wpk, w1_ss.at[dx], w_own if dx == 0 else None)
    for i in range(3):
        sent(w2_args(i)[0], w2_ss.at[i])
    for i in range(4):
        for k in range(4):
            sent(w3_args(i, k)[0], w3_ss.at[i, k])
    for k in range(2):
        for s in range(8):
            sent(cb.at[pl.ds(s * 4, 4), :, cot_cols(c, k)], f_ss.at[k, s])
    for st in range(6):
        for k in range(6):
            sent(y_args(st, k)[0], y_ss.at[st, k])
        for k in range(3):
            sent(z_args(st, k)[0], z_ss.at[st, k])
        for kc in range(2):
            sent(x_args(st, kc)[0], x_ss.at[st, kc], x_own(st, kc))


def local(query_in, key_in, value_in, cotangent, out_weight):
    any_spec = pl.BlockSpec(memory_space=pl.ANY)
    vmem_spec = pl.BlockSpec(memory_space=pltpu.VMEM)
    dma = pltpu.SemaphoreType.DMA
    act = jax.ShapeDtypeStruct((4, 64, HD), BF16)
    tok = (FRAMES, POS, HALF)
    gq, gk, gv, gw = pl.pallas_call(
        kernel,
        out_shape=(act, act, act, jax.ShapeDtypeStruct((12, D), F32)),
        in_specs=[any_spec] * 4 + [vmem_spec],
        out_specs=(any_spec, any_spec, any_spec, vmem_spec),
        scratch_shapes=[
            pltpu.VMEM(tok, BF16), pltpu.VMEM(tok, BF16), pltpu.VMEM(tok, BF16),
            pltpu.VMEM((FRAMES, POS, D), BF16),
            pltpu.VMEM((16, PK), F32),
            pltpu.VMEM((16, PK), BF16),
            pltpu.VMEM((2, 4, 4, 32, PK), BF16),
            pltpu.VMEM((HALF, D), BF16),
            pltpu.VMEM((HEADS, TOK, TOK), F32),
            pltpu.VMEM((TOK, HALF), BF16),
            pltpu.VMEM((3, 2, ROWS, TOK), BF16),
            pltpu.VMEM((3, ROWS, NAT), BF16),
            pltpu.VMEM((4, NAT, ROWS), BF16),
            pltpu.VMEM((6, 4, 128, COL), BF16),
            pltpu.VMEM((6, 2, 64, COL), BF16),
            pltpu.VMEM((6, 2, 128, COL), BF16),
            pltpu.VMEM((6, 128, COL), BF16),
            pltpu.VMEM((6, 32, COL), BF16),
            pltpu.VMEM((6, 2, 32, COL), BF16),
            pltpu.VMEM((6, 32, COL), BF16),
            pltpu.VMEM((3, 4, 16, COL), BF16),
            pltpu.VMEM((TOK, HALF), BF16),
            pltpu.VMEM(tok, BF16), pltpu.VMEM(tok, BF16), pltpu.VMEM(tok, BF16),
            dma((8, 8)), dma((8, 8)), dma((2, 8)), dma((2, 8)),
            dma((4,)), dma((4,)), dma((3,)), dma((3,)), dma((4, 4)), dma((4, 4)),
            dma((6, 6)), dma((6, 6)), dma((6, 3)), dma((6, 3)), dma((6, 2)), dma((3, 4)),
            dma((6, 8)), dma((6, 8)),
        ],
        compiler_params=pltpu.CompilerParams(
            collective_id=0, has_side_effects=True, vmem_limit_bytes=58 * 2**20
        ),
    )(
        query_in.reshape(4, 64, HD), key_in.reshape(4, 64, HD), value_in.reshape(4, 64, HD),
        cotangent.reshape(4, 64, D), out_weight,
    )
    shape = (1, 4, 64, HD)
    return gq.reshape(shape), gk.reshape(shape), gv.reshape(shape), gw


def solution(mesh):
    act, rows = P("dp", "seq", None, None), P(("seq", "dp"), None)
    return jax.shard_map(
        local, mesh=mesh, in_specs=(act, act, act, act, rows), out_specs=(act, act, act, rows),
        check_vma=False,
    )
```
